256 devices in a mesh: dp: 64 (over x, z, core), tensor: 4 (over y).
Axes of the slice: x: 4, y: 4, z: 8, core: 2. Of those that a mesh axis runs over, the one named last changes fastest.
Arguments:
- features: bfloat16 [1, 16384, 4096], P(None, 'dp', 'tensor'), may hold values from -6 to 6
- cotangent: bfloat16 [1, 16384, 11008], P(None, 'dp', 'tensor'), may hold values from -16 to 16
- basis: bfloat16 [1, 4096, 512], P(None, 'tensor'), may hold values from -0.25 to 0.25
- first_moment: float32 [1, 11008, 512], P(None, ('tensor', 'dp')), may hold values from -0.06 to 0.06
- second_moment: float32 [1, 11008, 512], P(None, ('tensor', 'dp')), may hold values from 1e-07 to 1e-05
Outputs:
- new_first: float32 [1, 11008, 512], P(None, ('tensor', 'dp'))
- new_second: float32 [1, 11008, 512], P(None, ('tensor', 'dp'))
- weight_change: bfloat16 [1, 4096, 4, 2752], P(None, 'tensor', None, 'dp')
The draws below stay inside these ranges and needn't reach their ends.
All inputs are finite; a program needn't handle non-finite values.
Results may differ from the reference program's by a relative error of at most 0.0059.
Values may be sent and summed in bfloat16 or wider, within the bound.
No kernel may reach another device: no remote copies, remote signals or barrier semaphores. Data moves between devices by JAX's collectives and lax.ppermute only.
A program may use at most 64 MiB of HBM per device.

```python
import math
import jax
import jax.numpy as jnp

D = 4096
FF = 11008
R = 512
LAYERS = 1
TOKENS = 16384
N_TENSOR = 4


def strengthened(result, own_key, source, target, parts, factor):
    def block_of(position):
        return (jnp.arange(result.shape[position]) // (result.shape[position] // parts)).reshape((-1,) + (1,) * (result.ndim - 1 - position))

    one_side = jax.random.permutation(own_key, parts)[block_of(target)]
    other_side = (block_of(target) + parts // 2) % parts
    return jnp.where((block_of(source) == one_side) | (block_of(source) == other_side), factor * result, result)


def shard_levels(stream_key, extent, cuts, least, high):
    loudness, own = 1.0, jax.random.fold_in(stream_key, 6)
    for position, parts in cuts:
        heights = jnp.exp(jax.random.uniform(jax.random.fold_in(own, position), (parts,), jnp.float32, least / len(cuts), high / len(cuts)))
        loudness = loudness * jnp.repeat(heights, extent[position] // parts).reshape([-1 if axis == position else 1 for axis in range(len(extent))])
    return loudness


def scatter_about(stream_key, extent, deviation, most, split=(), dtype=jnp.bfloat16):
    loudness = shard_levels(stream_key, extent, split, -0.22, 0.18) if split else 1.0
    drawn = jax.random.normal(stream_key, extent, jnp.float32) * deviation * loudness
    return jnp.minimum(jnp.maximum(drawn, -most), most).astype(dtype)


def gaussian_with(rng, dims, deviation, limit, shards, heavy, held_as=jnp.bfloat16):
    result = deviation * jax.random.normal(rng, dims, jnp.float32)
    if shards:
        result = result * shard_levels(rng, dims, shards, -0.22, 0.18)
    return jnp.clip(strengthened(result, jax.random.fold_in(rng, 3), *heavy), -limit, limit).astype(held_as)


def setup_inputs(seed: int = 0) -> dict:
    key_of = jax.random.split(jax.random.key(seed), 6)
    return {
        "features": scatter_about(key_of[0], (LAYERS, TOKENS, D), 1.0, 6.0, ((1, 64), (2, 4))),
        "cotangent": gaussian_with(key_of[1], (LAYERS, TOKENS, FF), 1.0, 16.0, ((1, 64), (2, 4)), (1, 2, 64, 4.0)),
        "basis": scatter_about(key_of[2], (LAYERS, D, R), R ** -0.5, 0.25, ((1, 4),)),
        "first_moment": scatter_about(key_of[3], (LAYERS, FF, R), 0.01, 0.06, ((1, 256),), jnp.float32),
        "second_moment": jnp.clip(jnp.exp(math.log(9.999999747378752e-06) - 4.6051701 * jax.random.uniform(key_of[4], (LAYERS, FF, R), jnp.float32) ** shard_levels(key_of[4], (LAYERS, FF, R), ((1, 256),), -0.2, 0.2)), 1.0000000116860974e-07, 9.999999747378752e-06),
    }


def reference(features, cotangent, basis, first_moment, second_moment):
    firsts = []
    seconds = []
    changes = []
    for layer in range(LAYERS):
        projected = jnp.dot(features[layer], basis[layer], preferred_element_type=jnp.float32).astype(jnp.bfloat16)
        low_rank = jnp.dot(cotangent[layer].T, projected, preferred_element_type=jnp.float32) / TOKENS
        first = 0.9 * first_moment[layer] + 0.1 * low_rank
        second = 0.999 * second_moment[layer] + 0.001 * low_rank * low_rank
        update = (first / (1.0 - 0.9 ** 10) / (jnp.sqrt(second / (1.0 - 0.999 ** 10)) + 1e-08)).astype(jnp.bfloat16)
        change = jnp.dot(basis[layer], update.T, preferred_element_type=jnp.float32).astype(jnp.bfloat16)
        firsts.append(first)
        seconds.append(second)
        changes.append(change.reshape(D, N_TENSOR, FF // N_TENSOR))
    return (jnp.stack(firsts), jnp.stack(seconds), jnp.stack(changes))
```

```python
import functools

import jax
import jax.numpy as jnp
from jax import lax
from jax.experimental import pallas as pl
from jax.experimental.pallas import tpu as pltpu
from jax.sharding import PartitionSpec as P

NX, NZ, NCORE, NY = 4, 8, 2, 4
OWNED, PADDED = 43, 48
BF, F32 = jnp.bfloat16, jnp.float32

Z_ORDER = (7, 3, 5, 1, 6, 2, 4, 0)
X_ORDER = {0: (2, 1, 3, 0), 1: (2, 3, 1, 0)}
X_STEPS = {0: (1, 3), 1: (3, 1)}


def send_dp(value, move):
    pairs = []
    for d in range(NX * NZ * NCORE):
        x, z, c = d // (NZ * NCORE), (d // NCORE) % NZ, d % NCORE
        x, z, c = move(x, z, c)
        pairs.append((d, (x * NZ + z) * NCORE + c))
    return lax.ppermute(value, "dp", pairs)


def swap_core(value):
    return send_dp(value, lambda x, z, c: (x, z, 1 - c))


def swap_x(value, m):
    return send_dp(value, lambda x, z, c: (x ^ m, z, c))


def swap_z(value, m, shift):
    return send_dp(value, lambda x, z, c: (x, (((z + shift) % NZ) ^ m) - shift & (NZ - 1), c))


def swap_y(value, m):
    return lax.ppermute(value, "tensor", [(y, y ^ m) for y in range(NY)])


def arrange_kernel(order_ref, core_ref, source, a_send, a_keep, b_send, b_keep, blocks):
    rows = source.shape[0]

    def unpack(core):
        for n in range(NX * NZ):
            first = (2 * n + core) * OWNED
            low = first // 16 * 16
            high = min(rows, -(-(first + PADDED) // 16) * 16)
            piece = source[low:high, :].astype(F32)
            piece = piece[first - low : min(first - low + PADDED, high - low), :]
            if piece.shape[0] < PADDED:
                fill = jnp.zeros((PADDED - piece.shape[0], piece.shape[1]), F32)
                piece = jnp.concatenate([piece, fill], axis=0)
            blocks[n] = piece.astype(BF)

    for core in range(NCORE):
        pl.when(core_ref[0] == core)(functools.partial(unpack, core))
    half = NX * NZ // 2
    for k, out in enumerate((a_send, a_keep, b_send, b_keep)):
        for i in range(half):
            out[i * PADDED : (i + 1) * PADDED, :] = blocks[order_ref[k * half + i]]


def arrange(order, core, source):
    half = NX * NZ // 2 * PADDED
    shape = jax.ShapeDtypeStruct((half, source.shape[1]), BF)
    vmem = pl.BlockSpec(memory_space=pltpu.VMEM)
    smem = pl.BlockSpec(memory_space=pltpu.SMEM)
    return pl.pallas_call(
        arrange_kernel,
        out_shape=[shape] * 4,
        in_specs=[smem, smem, vmem],
        out_specs=[vmem] * 4,
        scratch_shapes=[pltpu.VMEM((NX * NZ, PADDED, source.shape[1]), BF)],
        compiler_params=pltpu.CompilerParams(vmem_limit_bytes=16 * 1024 * 1024),
        cost_estimate=pl.CostEstimate(flops=0, bytes_accessed=8 * 1024 * 1024, transcendentals=0),
    )(order, core, source)


def dot(a, b):
    return lax.dot_general(a, b, (((1,), (0,)), ((), ())), preferred_element_type=F32)


def local(features, cotangent, basis, first_moment, second_moment):
    rank = basis.shape[2]
    half = rank // 2
    scale = 1.0 / (features.shape[1] * lax.axis_size("dp"))
    dp = lax.axis_index("dp")
    core, z, x = dp % NCORE, (dp // NCORE) % NZ, dp // (NCORE * NZ)
    y = lax.axis_index("tensor")

    columns = cotangent[0].T
    other_columns = swap_core(columns)
    order = []
    for part in range(2):
        zz = jnp.array(Z_ORDER, jnp.int32) ^ ((z + part) % NZ)
        zz = (zz + NZ - part) % NZ
        xx = jnp.array(X_ORDER[part], jnp.int32) ^ x
        order.append((xx[:, None] * NZ + zz[None, :]).reshape(-1))
    order = jnp.concatenate(order)
    core1 = core.reshape(1)
    mine = arrange(order, core1, columns)
    theirs = arrange(order, core1, other_columns)

    partial = dot(features[0], basis[0])
    halves = [partial[:, :half], partial[:, half:]]
    for step in range(2):
        came = [swap_y(halves[p].astype(BF), X_STEPS[p][step]) for p in range(2)]
        halves = [h + c.astype(F32) for h, c in zip(halves, came)]
    projected = jnp.concatenate([h.astype(BF) for h in halves], axis=1)
    other_projected = swap_core(projected)

    def term(k, p):
        lanes = slice(p * half, (p + 1) * half)
        return dot(mine[k], projected[:, lanes]) + dot(theirs[k], other_projected[:, lanes])

    sends = [term(2 * p, p).astype(BF) for p in range(2)]
    came = [swap_x(sends[p], X_STEPS[p][0]) for p in range(2)]
    kept = [term(2 * p + 1, p) for p in range(2)]
    kept = [k + c.astype(F32) for k, c in zip(kept, came)]
    n = NZ * PADDED
    came = [swap_x(kept[p][:n].astype(BF), X_STEPS[p][1]) for p in range(2)]
    kept = [k[n:] + c.astype(F32) for k, c in zip(kept, came)]
    for m in (1, 2, 4):
        n //= 2
        came = [swap_z(kept[p][:n].astype(BF), m, p) for p in range(2)]
        kept = [k[n:] + c.astype(F32) for k, c in zip(kept, came)]

    grads = (jnp.concatenate([k[:OWNED] for k in kept], axis=1) * scale)[None]
    new_first = 0.9 * first_moment + 0.1 * grads
    new_second = 0.999 * second_moment + 0.001 * grads * grads
    update = (
        new_first / (1.0 - 0.9**10) / (jnp.sqrt(new_second / (1.0 - 0.999**10)) + 1e-08)
    ).astype(BF)[0]

    around = [update] + [swap_y(update, m) for m in (1, 2, 3)]
    ordered = jnp.stack([lax.select_n(y ^ a, *around) for a in range(NY)])
    change = jnp.einsum("dr,acr->dac", basis[0], ordered, preferred_element_type=F32)
    return (new_first, new_second, change.astype(BF)[None])


def solution(mesh):
    return jax.shard_map(
        local,
        mesh=mesh,
        in_specs=(
            P(None, "dp", "tensor"),
            P(None, "dp", "tensor"),
            P(None, "tensor", None),
            P(None, ("tensor", "dp"), None),
            P(None, ("tensor", "dp"), None),
        ),
        out_specs=(
            P(None, ("tensor", "dp"), None),
            P(None, ("tensor", "dp"), None),
            P(None, "tensor", None, "dp"),
        ),
        check_vma=False,
    )
```

```python
import functools

import jax
import jax.numpy as jnp
from jax import lax
from jax.experimental import pallas as pl
from jax.experimental.pallas import tpu as pltpu
from jax.sharding import PartitionSpec as P

NX, NZ, NCORE, NY = 4, 8, 2, 4
OWNED, PADDED = 43, 48
BF, F32 = jnp.bfloat16, jnp.float32

Z_ORDER = (6, 1, 4, 7, 2, 5, 0, 3)
UP, DOWN = 2 * PADDED, 5 * PADDED


def send_dp(value, move):
    pairs = []
    for d in range(NX * NZ * NCORE):
        x, z, c = d // (NZ * NCORE), (d // NCORE) % NZ, d % NCORE
        x, z, c = move(x, z, c)
        pairs.append((d, (x * NZ + z) * NCORE + c))
    return lax.ppermute(value, "dp", pairs)


def swap_core(value):
    return send_dp(value, lambda x, z, c: (x, z, 1 - c))


def swap_x(value, m):
    return send_dp(value, lambda x, z, c: (x ^ m, z, c))


def shift_z(value, k):
    return send_dp(value, lambda x, z, c: (x, (z + k) % NZ, c))


def swap_y(value, m):
    return lax.ppermute(value, "tensor", [(y, y ^ m) for y in range(NY)])


def arrange_kernel(order_ref, core_ref, *refs):
    sources, (other, mine, blocks) = refs[:NX], refs[NX:]
    rows, tokens = sources[0].shape
    for s, source in enumerate(sources):
        for n in range(NZ * NCORE):
            first = n * OWNED
            low = first // 16 * 16
            high = min(rows, -(-(first + PADDED) // 16) * 16)
            piece = source[low:high, :].astype(F32)
            piece = piece[first - low : min(first - low + PADDED, high - low), :]
            if piece.shape[0] < PADDED:
                fill = jnp.zeros((PADDED - piece.shape[0], tokens), F32)
                piece = jnp.concatenate([piece, fill], axis=0)
            blocks[n, :, s * tokens : (s + 1) * tokens] = piece.astype(BF)
    core = core_ref[0]
    for i in range(NZ):
        place = pl.ds(i * PADDED, PADDED)
        other[place, :] = blocks[order_ref[i] * NCORE + 1 - core]
        mine[place, :] = blocks[order_ref[i] * NCORE + core]


def arrange(order, core, sources):
    rows, tokens = sources[0].shape
    shape = jax.ShapeDtypeStruct((NZ * PADDED, NX * tokens), BF)
    vmem = pl.BlockSpec(memory_space=pltpu.VMEM)
    smem = pl.BlockSpec(memory_space=pltpu.SMEM)
    return pl.pallas_call(
        arrange_kernel,
        out_shape=[shape] * 2,
        in_specs=[smem, smem] + [vmem] * NX,
        out_specs=[vmem] * 2,
        scratch_shapes=[pltpu.VMEM((NZ * NCORE, PADDED, NX * tokens), BF)],
        compiler_params=pltpu.CompilerParams(vmem_limit_bytes=16 * 1024 * 1024),
        cost_estimate=pl.CostEstimate(flops=0, bytes_accessed=8 * 1024 * 1024, transcendentals=0),
    )(order, core, *sources)


def dot(a, b):
    return lax.dot_general(a, b, (((1,), (0,)), ((), ())), preferred_element_type=F32)


def local(features, cotangent, basis, first_moment, second_moment):
    scale = 1.0 / (features.shape[1] * lax.axis_size("dp"))
    dp = lax.axis_index("dp")
    core, z, x = dp % NCORE, (dp // NCORE) % NZ, dp // (NCORE * NZ)
    y = lax.axis_index("tensor")

    columns = cotangent[0].T.reshape(NX, -1, cotangent.shape[1])
    pieces = [lax.dynamic_index_in_dim(columns, x ^ m, 0, keepdims=False) for m in range(NX)]
    pieces = pieces[:1] + [swap_x(pieces[m], m) for m in range(1, NX)]

    partial = dot(features[0], basis[0])
    sent = partial.astype(BF)
    came = [swap_y(sent, m).astype(F32) for m in range(1, NY)]
    projected = (partial + came[0] + came[1] + came[2]).astype(BF)
    projected = jnp.concatenate([projected] + [swap_x(projected, m) for m in range(1, NX)], axis=0)

    order = (jnp.array(Z_ORDER, jnp.int32) + z) % NZ
    other, mine = arrange(order, core.reshape(1), pieces)
    came = swap_core(dot(other, projected).astype(BF))
    term = dot(mine, projected) + came.astype(F32)
    lower = shift_z(term[:UP].astype(BF), 1).astype(F32)
    upper = shift_z(term[UP:DOWN].astype(BF), -1).astype(F32)
    keep = term[DOWN:] + upper
    keep = [
        keep[:PADDED] + lower[:PADDED],
        keep[PADDED:UP] + lower[PADDED:],
        keep[UP:],
    ]
    lower = shift_z(keep[0].astype(BF), -3).astype(F32)
    upper = shift_z(keep[2].astype(BF), 3).astype(F32)
    total = keep[1] + lower + upper

    grads = (total[:OWNED] * scale)[None]
    new_first = 0.9 * first_moment + 0.1 * grads
    new_second = 0.999 * second_moment + 0.001 * grads * grads
    update = (
        new_first / (1.0 - 0.9**10) / (jnp.sqrt(new_second / (1.0 - 0.999**10)) + 1e-08)
    ).astype(BF)[0]

    around = [update] + [swap_y(update, m) for m in (1, 2, 3)]
    ordered = jnp.stack([lax.select_n(y ^ a, *around) for a in range(NY)])
    change = jnp.einsum("dr,acr->dac", basis[0], ordered, preferred_element_type=F32)
    return (new_first, new_second, change.astype(BF)[None])


def solution(mesh):
    return jax.shard_map(
        local,
        mesh=mesh,
        in_specs=(
            P(None, "dp", "tensor"),
            P(None, "dp", "tensor"),
            P(None, "tensor", None),
            P(None, ("tensor", "dp"), None),
            P(None, ("tensor", "dp"), None),
        ),
        out_specs=(
            P(None, ("tensor", "dp"), None),
            P(None, ("tensor", "dp"), None),
            P(None, "tensor", None, "dp"),
        ),
        check_vma=False,
    )
```

```python
import functools

import jax
import jax.numpy as jnp
from jax import lax
from jax.experimental import pallas as pl
from jax.experimental.pallas import tpu as pltpu
from jax.sharding import PartitionSpec as P

NX, NZ, NCORE, NY = 4, 8, 2, 4
OWNED, PADDED = 43, 48
CHUNKS = 2
BF, F32 = jnp.bfloat16, jnp.float32

Z_ORDER = (6, 1, 4, 7, 2, 5, 0, 3)
UP, DOWN = 2 * PADDED, 5 * PADDED


def send_dp(value, move):
    pairs = []
    for d in range(NX * NZ * NCORE):
        x, z, c = d // (NZ * NCORE), (d // NCORE) % NZ, d % NCORE
        x, z, c = move(x, z, c)
        pairs.append((d, (x * NZ + z) * NCORE + c))
    return lax.ppermute(value, "dp", pairs)


def swap_core(value):
    return send_dp(value, lambda x, z, c: (x, z, 1 - c))


def swap_x(value, m):
    return send_dp(value, lambda x, z, c: (x ^ m, z, c))


def shift_z(value, k):
    return send_dp(value, lambda x, z, c: (x, (z + k) % NZ, c))


def swap_y(value, m):
    return lax.ppermute(value, "tensor", [(y, y ^ m) for y in range(NY)])


def arrange_kernel(order_ref, core_ref, own, came, *refs):
    outs, blocks = refs[:NX], refs[NX]
    rows, tokens = own.shape

    def unpack(core):
        for s, source in enumerate((own, came)):
            for n in range(NX * NZ):
                first = (NCORE * n + core) * OWNED
                low = first // 16 * 16
                high = min(rows, -(-(first + PADDED) // 16) * 16)
                piece = source[low:high, :].astype(F32)
                piece = piece[first - low : min(first - low + PADDED, high - low), :]
                if piece.shape[0] < PADDED:
                    fill = jnp.zeros((PADDED - piece.shape[0], tokens), F32)
                    piece = jnp.concatenate([piece, fill], axis=0)
                blocks[n, :, s * tokens : (s + 1) * tokens] = piece.astype(BF)

    for core in range(NCORE):
        pl.when(core_ref[0] == core)(functools.partial(unpack, core))
    for m, out in enumerate(outs):
        for i in range(NZ):
            out[pl.ds(i * PADDED, PADDED), :] = blocks[order_ref[m * NZ + i]]


def arrange(order, core, own, came):
    tokens = own.shape[1]
    shape = jax.ShapeDtypeStruct((NZ * PADDED, NCORE * tokens), BF)
    vmem = pl.BlockSpec(memory_space=pltpu.VMEM)
    smem = pl.BlockSpec(memory_space=pltpu.SMEM)
    return pl.pallas_call(
        arrange_kernel,
        out_shape=[shape] * NX,
        in_specs=[smem, smem, vmem, vmem],
        out_specs=[vmem] * NX,
        scratch_shapes=[pltpu.VMEM((NX * NZ, PADDED, NCORE * tokens), BF)],
        compiler_params=pltpu.CompilerParams(vmem_limit_bytes=16 * 1024 * 1024),
        cost_estimate=pl.CostEstimate(flops=0, bytes_accessed=8 * 1024 * 1024, transcendentals=0),
    )(order, core, own, came)


def dot(a, b):
    return lax.dot_general(a, b, (((1,), (0,)), ((), ())), preferred_element_type=F32)


def local(features, cotangent, basis, first_moment, second_moment):
    scale = 1.0 / (features.shape[1] * lax.axis_size("dp"))
    dp = lax.axis_index("dp")
    core, z, x = dp % NCORE, (dp // NCORE) % NZ, dp // (NCORE * NZ)
    y = lax.axis_index("tensor")

    columns = cotangent[0].T
    other_columns = swap_core(columns)
    blocks_x = jnp.arange(NX, dtype=jnp.int32) ^ x
    blocks_z = (jnp.array(Z_ORDER, jnp.int32) + z) % NZ
    order = (blocks_x[:, None] * NZ + blocks_z[None, :]).reshape(-1)
    parts = arrange(order, core.reshape(1), columns, other_columns)

    lanes = basis.shape[2] // CHUNKS
    projected = []
    for c in range(CHUNKS):
        partial = dot(features[0], basis[0, :, c * lanes : (c + 1) * lanes])
        sent = partial.astype(BF)
        came = [swap_y(sent, m).astype(F32) for m in range(1, NY)]
        projected.append((partial + came[0] + came[1] + came[2]).astype(BF))
    projected[0], parts = lax.optimization_barrier((projected[0], parts))

    terms = []
    for c in range(CHUNKS):
        both = jnp.concatenate([projected[c], swap_core(projected[c])], axis=0)
        came = [swap_x(dot(parts[m], both).astype(BF), m) for m in range(1, NX)]
        term = dot(parts[0], both)
        for value in came:
            term = term + value.astype(F32)
        terms.append(term)
    term = jnp.concatenate(terms, axis=1)

    lower = shift_z(term[:UP].astype(BF), 1).astype(F32)
    upper = shift_z(term[UP:DOWN].astype(BF), -1).astype(F32)
    keep = term[DOWN:] + upper
    keep = [
        keep[:PADDED] + lower[:PADDED],
        keep[PADDED:UP] + lower[PADDED:],
        keep[UP:],
    ]
    lower = shift_z(keep[0].astype(BF), -3).astype(F32)
    upper = shift_z(keep[2].astype(BF), 3).astype(F32)
    total = keep[1] + lower + upper

    grads = (total[:OWNED] * scale)[None]
    new_first = 0.9 * first_moment + 0.1 * grads
    new_second = 0.999 * second_moment + 0.001 * grads * grads
    update = (
        new_first / (1.0 - 0.9**10) / (jnp.sqrt(new_second / (1.0 - 0.999**10)) + 1e-08)
    ).astype(BF)[0]

    around = [update] + [swap_y(update, m) for m in (1, 2, 3)]
    ordered = jnp.stack([lax.select_n(y ^ a, *around) for a in range(NY)])
    change = jnp.einsum("dr,acr->dac", basis[0], ordered, preferred_element_type=F32)
    return (new_first, new_second, change.astype(BF)[None])


def solution(mesh):
    return jax.shard_map(
        local,
        mesh=mesh,
        in_specs=(
            P(None, "dp", "tensor"),
            P(None, "dp", "tensor"),
            P(None, "tensor", None),
            P(None, ("tensor", "dp"), None),
            P(None, ("tensor", "dp"), None),
        ),
        out_specs=(
            P(None, ("tensor", "dp"), None),
            P(None, ("tensor", "dp"), None),
            P(None, "tensor", None, "dp"),
        ),
        check_vma=False,
    )
```

```python
import jax
import jax.numpy as jnp
from jax import lax
from jax.experimental import pallas as pl
from jax.experimental.layout import Layout, with_layout_constraint
from jax.experimental.pallas import tpu as pltpu
from jax.sharding import PartitionSpec as P

NX, NZ, NCORE, NY = 4, 8, 2, 4
OWNED = 43
CHIP, PADDED = NCORE * OWNED, 88
BF, F32 = jnp.bfloat16, jnp.float32

Z_ORDER = (-2, 1, -4, -1, 2, 3, 0, -3)
FIRST, SECOND = 2 * PADDED, 5 * PADDED
X_ORDER = ((2, 1, 3, 0), (2, 3, 1, 0))
PAIRS = ((1, 3), (3, 1))


def send(value, move):
    pairs = []
    for d in range(NX * NZ * NCORE * NY):
        x, z, c, y = d // (NZ * NCORE * NY), d // (NCORE * NY) % NZ, d // NY % NCORE, d % NY
        x, z, c, y = move(x, z, c, y)
        pairs.append((d, ((x * NZ + z) * NCORE + c) * NY + y))
    value = with_layout_constraint(value, Layout(major_to_minor=(0, 1)))
    return lax.ppermute(value, ("dp", "tensor"), pairs)


def swap_core(value):
    return send(value, lambda x, z, c, y: (x, z, 1 - c, y))


def swap_x(value, step):
    return send(value, lambda x, z, c, y: (x ^ PAIRS[c][step], z, c, y))


def swap_y(value, step):
    return send(value, lambda x, z, c, y: (x, z, c, y ^ PAIRS[c][step]))


def swap_z(value, k):
    return send(value, lambda x, z, c, y: (x, (z + k * (1 - 2 * (z % 2))) % NZ, c, y))


def around_y(value, m):
    return send(value, lambda x, z, c, y: (x, z, c, y ^ m))


def arrange_kernel(order_ref, own, came, first, second, blocks):
    rows, tokens = own.shape
    for s, source in enumerate((own, came)):
        for n in range(NX * NZ):
            start = n * CHIP
            low = start // 16 * 16
            high = min(rows, -(-(start + PADDED) // 16) * 16)
            piece = source[low:high, :].astype(F32)
            piece = piece[start - low : min(start - low + PADDED, high - low), :]
            if piece.shape[0] < PADDED:
                fill = jnp.zeros((PADDED - piece.shape[0], tokens), F32)
                piece = jnp.concatenate([piece, fill], axis=0)
            blocks[n, :, s * tokens : (s + 1) * tokens] = piece
    half = NX * NZ // 2
    for k, out in enumerate((first, second)):
        for i in range(0, half, 2):
            pair = [blocks[order_ref[k * half + i + j]] for j in range(2)]
            out[i * PADDED : (i + 2) * PADDED, :] = jnp.concatenate(pair, axis=0).astype(BF)


def arrange(order, own, came):
    tokens = own.shape[1]
    shape = jax.ShapeDtypeStruct((NX * NZ // 2 * PADDED, NCORE * tokens), BF)
    vmem = pl.BlockSpec(memory_space=pltpu.VMEM)
    smem = pl.BlockSpec(memory_space=pltpu.SMEM)
    return pl.pallas_call(
        arrange_kernel,
        out_shape=[shape] * 2,
        in_specs=[smem, vmem, vmem],
        out_specs=[vmem] * 2,
        scratch_shapes=[pltpu.VMEM((NX * NZ, PADDED, NCORE * tokens), F32)],
        compiler_params=pltpu.CompilerParams(vmem_limit_bytes=20 * 1024 * 1024),
        cost_estimate=pl.CostEstimate(flops=0, bytes_accessed=8 * 1024 * 1024, transcendentals=0),
    )(order, own, came)


def dot(a, b):
    out = lax.dot_general(a, b, (((1,), (0,)), ((), ())), preferred_element_type=F32)
    return with_layout_constraint(out, Layout(major_to_minor=(0, 1)))


def local(features, cotangent, basis, first_moment, second_moment):
    lanes = basis.shape[2] // NCORE
    scale = 1.0 / (features.shape[1] * lax.axis_size("dp"))
    dp = lax.axis_index("dp")
    core, z, x = dp & 1, (dp >> 1) & (NZ - 1), dp >> 4
    y = lax.axis_index("tensor")

    columns = cotangent[0].T
    other_columns = swap_core(columns)
    up = 1 - 2 * (z & 1)
    blocks_z = (z + up * jnp.array(Z_ORDER, jnp.int32)) & (NZ - 1)
    blocks_x = x ^ jnp.where(core == 0, jnp.array(X_ORDER[0]), jnp.array(X_ORDER[1]))
    order = (blocks_x[:, None] * NZ + blocks_z[None, :]).reshape(-1)
    first, second = arrange(order, columns, other_columns)

    def lanes_of(c):
        return lax.dynamic_slice(basis[0], (0, c * lanes), (basis.shape[1], lanes))

    theirs = swap_core(dot(features[0], lanes_of(1 - core)).astype(BF))
    partial = jnp.concatenate([dot(features[0], lanes_of(core)), theirs.astype(F32)], axis=0)
    for step in range(2):
        partial = partial + swap_y(partial.astype(BF), step).astype(F32)
    projected, first, second = lax.optimization_barrier((partial.astype(BF), first, second))

    came = swap_x(dot(first, projected).astype(BF), 0)
    term = dot(second, projected) + came.astype(F32)
    rows = NZ * PADDED
    term = term[rows:] + swap_x(term[:rows].astype(BF), 1).astype(F32)
    came = swap_z(term[:FIRST].astype(BF), 1).astype(F32)
    more = swap_z(term[FIRST:SECOND].astype(BF), -1).astype(F32)
    keep = term[SECOND:] + more
    hub_a, own, hub_b = keep[:PADDED], keep[PADDED:FIRST], keep[FIRST:]
    hub_a, own = hub_a + came[:PADDED], own + came[PADDED:]
    came = swap_z(hub_a.astype(BF), 3).astype(F32)
    own = own + swap_z(hub_b.astype(BF), -3).astype(F32) + came
    mine, other = own[:OWNED], own[OWNED:CHIP]
    came = swap_core(jnp.where(core == 0, other, mine))
    mine = jnp.where(core == 0, mine, other)
    grads = jnp.concatenate(
        [jnp.where(core == 0, mine, came), jnp.where(core == 0, came, mine)], axis=1
    )

    grads = (grads * scale)[None]
    new_first = 0.9 * first_moment + 0.1 * grads
    new_second = 0.999 * second_moment + 0.001 * grads * grads
    update = (
        new_first / (1.0 - 0.9**10) / (jnp.sqrt(new_second / (1.0 - 0.999**10)) + 1e-08)
    ).astype(BF)[0]

    around = [update] + [around_y(update, m) for m in (1, 2, 3)]
    ordered = jnp.stack([lax.select_n(y ^ a, *around) for a in range(NY)])
    change = jnp.einsum("dr,acr->dac", basis[0], ordered, preferred_element_type=F32)
    return (new_first, new_second, change.astype(BF)[None])


def solution(mesh):
    return jax.shard_map(
        local,
        mesh=mesh,
        in_specs=(
            P(None, "dp", "tensor"),
            P(None, "dp", "tensor"),
            P(None, "tensor", None),
            P(None, ("tensor", "dp"), None),
            P(None, ("tensor", "dp"), None),
        ),
        out_specs=(
            P(None, ("tensor", "dp"), None),
            P(None, ("tensor", "dp"), None),
            P(None, "tensor", None, "dp"),
        ),
        check_vma=False,
    )
```

```python
import jax
import jax.numpy as jnp
from jax import lax
from jax.experimental import pallas as pl
from jax.experimental.layout import Layout, with_layout_constraint
from jax.experimental.pallas import tpu as pltpu
from jax.sharding import PartitionSpec as P

NX, NZ, NCORE, NY = 4, 8, 2, 4
OWNED = 43
CHUNKS = 2
CHIP, PADDED = NCORE * OWNED, 88
BF, F32 = jnp.bfloat16, jnp.float32

Z_ORDER = (-2, 1, -4, -1, 2, 3, 0, -3)
FIRST, SECOND = 2 * PADDED, 5 * PADDED
X_ORDER = ((2, 1, 3, 0), (2, 3, 1, 0))
PAIRS = ((1, 3), (3, 1))


def send(value, move):
    pairs = []
    for d in range(NX * NZ * NCORE * NY):
        x, z, c, y = d // (NZ * NCORE * NY), d // (NCORE * NY) % NZ, d // NY % NCORE, d % NY
        x, z, c, y = move(x, z, c, y)
        pairs.append((d, ((x * NZ + z) * NCORE + c) * NY + y))
    value = with_layout_constraint(value, Layout(major_to_minor=(0, 1)))
    return lax.ppermute(value, ("dp", "tensor"), pairs)


def swap_core(value):
    return send(value, lambda x, z, c, y: (x, z, 1 - c, y))


def swap_x(value, step):
    return send(value, lambda x, z, c, y: (x ^ PAIRS[c][step], z, c, y))


def swap_y(value, step):
    return send(value, lambda x, z, c, y: (x, z, c, y ^ PAIRS[c][step]))


def swap_z(value, k):
    return send(value, lambda x, z, c, y: (x, (z + k * (1 - 2 * (z % 2))) % NZ, c, y))


def around_y(value, m):
    return send(value, lambda x, z, c, y: (x, z, c, y ^ m))


def arrange_kernel(order_ref, own, came, first, second, blocks):
    rows, tokens = own.shape
    for s, source in enumerate((own, came)):
        for n in range(NX * NZ):
            start = n * CHIP
            low = start // 16 * 16
            high = min(rows, -(-(start + PADDED) // 16) * 16)
            piece = source[low:high, :].astype(F32)
            piece = piece[start - low : min(start - low + PADDED, high - low), :]
            if piece.shape[0] < PADDED:
                fill = jnp.zeros((PADDED - piece.shape[0], tokens), F32)
                piece = jnp.concatenate([piece, fill], axis=0)
            blocks[n, :, s * tokens : (s + 1) * tokens] = piece
    half = NX * NZ // 2
    for k, out in enumerate((first, second)):
        for i in range(0, half, 2):
            pair = [blocks[order_ref[k * half + i + j]] for j in range(2)]
            out[i * PADDED : (i + 2) * PADDED, :] = jnp.concatenate(pair, axis=0).astype(BF)


def arrange(order, own, came):
    tokens = own.shape[1]
    shape = jax.ShapeDtypeStruct((NX * NZ // 2 * PADDED, NCORE * tokens), BF)
    vmem = pl.BlockSpec(memory_space=pltpu.VMEM)
    smem = pl.BlockSpec(memory_space=pltpu.SMEM)
    return pl.pallas_call(
        arrange_kernel,
        out_shape=[shape] * 2,
        in_specs=[smem, vmem, vmem],
        out_specs=[vmem] * 2,
        scratch_shapes=[pltpu.VMEM((NX * NZ, PADDED, NCORE * tokens), F32)],
        compiler_params=pltpu.CompilerParams(vmem_limit_bytes=20 * 1024 * 1024),
        cost_estimate=pl.CostEstimate(flops=0, bytes_accessed=8 * 1024 * 1024, transcendentals=0),
    )(order, own, came)


def dot(a, b):
    out = lax.dot_general(a, b, (((1,), (0,)), ((), ())), preferred_element_type=F32)
    return with_layout_constraint(out, Layout(major_to_minor=(0, 1)))


def local(features, cotangent, basis, first_moment, second_moment):
    lanes = basis.shape[2] // NCORE
    scale = 1.0 / (features.shape[1] * lax.axis_size("dp"))
    dp = lax.axis_index("dp")
    core, z, x = dp & 1, (dp >> 1) & (NZ - 1), dp >> 4
    y = lax.axis_index("tensor")

    columns = cotangent[0].T
    other_columns = swap_core(columns)
    up = 1 - 2 * (z & 1)
    blocks_z = (z + up * jnp.array(Z_ORDER, jnp.int32)) & (NZ - 1)
    blocks_x = x ^ jnp.where(core == 0, jnp.array(X_ORDER[0]), jnp.array(X_ORDER[1]))
    order = (blocks_x[:, None] * NZ + blocks_z[None, :]).reshape(-1)

    def lanes_of(c):
        return lax.dynamic_slice(basis[0], (0, c * lanes), (basis.shape[1], lanes))

    theirs = swap_core(dot(features[0], lanes_of(1 - core)).astype(BF))
    partial = jnp.concatenate([dot(features[0], lanes_of(core)), theirs.astype(F32)], axis=0)
    width = lanes // CHUNKS
    chunks = [partial[:, c * width : (c + 1) * width] for c in range(CHUNKS)]
    chunks = [p + swap_y(p.astype(BF), 0).astype(F32) for p in chunks]
    chunks, other_columns = lax.optimization_barrier((chunks, other_columns))
    first, second = arrange(order, columns, other_columns)
    chunks = [(p + swap_y(p.astype(BF), 1).astype(F32)).astype(BF) for p in chunks]
    chunks[0], first, second = lax.optimization_barrier((chunks[0], first, second))

    rows = NZ * PADDED
    terms = []
    for projected in chunks:
        came = swap_x(dot(first, projected).astype(BF), 0)
        term = dot(second, projected) + came.astype(F32)
        terms.append(term[rows:] + swap_x(term[:rows].astype(BF), 1).astype(F32))
    term = jnp.concatenate(terms, axis=1)
    came = swap_z(term[:FIRST].astype(BF), 1).astype(F32)
    more = swap_z(term[FIRST:SECOND].astype(BF), -1).astype(F32)
    keep = term[SECOND:] + more
    hub_a, own, hub_b = keep[:PADDED], keep[PADDED:FIRST], keep[FIRST:]
    hub_a, own = hub_a + came[:PADDED], own + came[PADDED:]
    came = swap_z(hub_a.astype(BF), 3).astype(F32)
    own = own + swap_z(hub_b.astype(BF), -3).astype(F32) + came
    mine, other = own[:OWNED], own[OWNED:CHIP]
    came = swap_core(jnp.where(core == 0, other, mine))
    mine = jnp.where(core == 0, mine, other)
    grads = jnp.concatenate(
        [jnp.where(core == 0, mine, came), jnp.where(core == 0, came, mine)], axis=1
    )

    grads = (grads * scale)[None]
    new_first = 0.9 * first_moment + 0.1 * grads
    new_second = 0.999 * second_moment + 0.001 * grads * grads
    update = (
        new_first / (1.0 - 0.9**10) / (jnp.sqrt(new_second / (1.0 - 0.999**10)) + 1e-08)
    ).astype(BF)[0]

    around = [update] + [around_y(update, m) for m in (1, 2, 3)]
    ordered = jnp.stack([lax.select_n(y ^ a, *around) for a in range(NY)])
    change = jnp.einsum("dr,acr->dac", basis[0], ordered, preferred_element_type=F32)
    return (new_first, new_second, change.astype(BF)[None])


def solution(mesh):
    return jax.shard_map(
        local,
        mesh=mesh,
        in_specs=(
            P(None, "dp", "tensor"),
            P(None, "dp", "tensor"),
            P(None, "tensor", None),
            P(None, ("tensor", "dp"), None),
            P(None, ("tensor", "dp"), None),
        ),
        out_specs=(
            P(None, ("tensor", "dp"), None),
            P(None, ("tensor", "dp"), None),
            P(None, "tensor", None, "dp"),
        ),
        check_vma=False,
    )
```

```python
import jax
import jax.numpy as jnp
from jax import lax
from jax.experimental import pallas as pl
from jax.experimental.layout import Layout, with_layout_constraint
from jax.experimental.pallas import tpu as pltpu
from jax.sharding import PartitionSpec as P

NX, NZ, NCORE, NY = 4, 8, 2, 4
OWNED = 43
CHUNKS = 2
CHIP, PADDED = NCORE * OWNED, 88
BF, F32 = jnp.bfloat16, jnp.float32

Z_ORDER = (-2, 1, -4, -1, 2, 3, 0, -3)
FIRST, SECOND = 2 * PADDED, 5 * PADDED
X_ORDER = ((2, 1, 3, 0), (2, 3, 1, 0))
PAIRS = ((1, 3), (3, 1))


def send(value, move):
    pairs = []
    for d in range(NX * NZ * NCORE * NY):
        x, z, c, y = d // (NZ * NCORE * NY), d // (NCORE * NY) % NZ, d // NY % NCORE, d % NY
        x, z, c, y = move(x, z, c, y)
        pairs.append((d, ((x * NZ + z) * NCORE + c) * NY + y))
    value = with_layout_constraint(value, Layout(major_to_minor=(0, 1)))
    return lax.ppermute(value, ("dp", "tensor"), pairs)


def swap_core(value):
    return send(value, lambda x, z, c, y: (x, z, 1 - c, y))


def swap_x(value, m):
    return send(value, lambda x, z, c, y: (x ^ m, z, c, y))


def swap_z(value, k):
    return send(value, lambda x, z, c, y: (x, (z + k * (1 - 2 * (z % 2))) % NZ, c, y))


def swap_y(value, m):
    return send(value, lambda x, z, c, y: (x, z, c, y ^ m))


def arrange_kernel(order_ref, own, came, *refs):
    outs, blocks = refs[:-1], refs[-1]
    rows, tokens = own.shape
    for s, source in enumerate((own, came)):
        for n in range(NX * NZ):
            start = n * CHIP
            low = start // 16 * 16
            high = min(rows, -(-(start + PADDED) // 16) * 16)
            piece = source[low:high, :].astype(F32)
            piece = piece[start - low : min(start - low + PADDED, high - low), :]
            if piece.shape[0] < PADDED:
                fill = jnp.zeros((PADDED - piece.shape[0], tokens), F32)
                piece = jnp.concatenate([piece, fill], axis=0)
            blocks[n, :, s * tokens : (s + 1) * tokens] = piece
    half = NX * NZ // 2
    for k, out in enumerate(outs):
        for i in range(0, half, 2):
            pair = [blocks[order_ref[k * half + i + j]] for j in range(2)]
            out[i * PADDED : (i + 2) * PADDED, :] = jnp.concatenate(pair, axis=0).astype(BF)


def arrange(order, own, came):
    tokens = own.shape[1]
    shape = jax.ShapeDtypeStruct((NX * NZ // 2 * PADDED, NCORE * tokens), BF)
    vmem = pl.BlockSpec(memory_space=pltpu.VMEM)
    smem = pl.BlockSpec(memory_space=pltpu.SMEM)
    return pl.pallas_call(
        arrange_kernel,
        out_shape=[shape] * 2 * CHUNKS,
        in_specs=[smem, vmem, vmem],
        out_specs=[vmem] * 2 * CHUNKS,
        scratch_shapes=[pltpu.VMEM((NX * NZ, PADDED, NCORE * tokens), F32)],
        compiler_params=pltpu.CompilerParams(vmem_limit_bytes=20 * 1024 * 1024),
        cost_estimate=pl.CostEstimate(flops=0, bytes_accessed=8 * 1024 * 1024, transcendentals=0),
    )(order, own, came)


def dot(a, b):
    out = lax.dot_general(a, b, (((1,), (0,)), ((), ())), preferred_element_type=F32)
    return with_layout_constraint(out, Layout(major_to_minor=(0, 1)))


def local(features, cotangent, basis, first_moment, second_moment):
    lanes = basis.shape[2] // NCORE
    scale = 1.0 / (features.shape[1] * lax.axis_size("dp"))
    dp = lax.axis_index("dp")
    core, z, x = dp & 1, (dp >> 1) & (NZ - 1), dp >> 4
    y = lax.axis_index("tensor")

    columns = cotangent[0].T
    other_columns = swap_core(columns)
    up = 1 - 2 * (z & 1)
    blocks_z = (z + up * jnp.array(Z_ORDER, jnp.int32)) & (NZ - 1)
    blocks_x = x ^ jnp.array(X_ORDER, jnp.int32).reshape(-1)
    order = (blocks_x[:, None] * NZ + blocks_z[None, :]).reshape(-1)

    def lanes_of(c):
        return lax.dynamic_slice(basis[0], (0, c * lanes), (basis.shape[1], lanes))

    theirs = swap_core(dot(features[0], lanes_of(1 - core)).astype(BF))
    partial = jnp.concatenate([dot(features[0], lanes_of(core)), theirs.astype(F32)], axis=0)
    width = lanes // CHUNKS
    chunks = [partial[:, c * width : (c + 1) * width] for c in range(CHUNKS)]
    chunks = [p + swap_y(p.astype(BF), m[0]).astype(F32) for p, m in zip(chunks, PAIRS)]
    chunks, other_columns = lax.optimization_barrier((chunks, other_columns))
    parts = arrange(order, columns, other_columns)
    chunks = [p + swap_y(p.astype(BF), m[1]).astype(F32) for p, m in zip(chunks, PAIRS)]
    chunks = [p.astype(BF) for p in chunks]
    chunks[0], parts = lax.optimization_barrier((chunks[0], parts))

    rows = NZ * PADDED
    terms = []
    for c, (projected, m) in enumerate(zip(chunks, PAIRS)):
        came = swap_x(dot(parts[2 * c], projected).astype(BF), m[0])
        term = dot(parts[2 * c + 1], projected) + came.astype(F32)
        terms.append(term[rows:] + swap_x(term[:rows].astype(BF), m[1]).astype(F32))
    term = jnp.concatenate(terms, axis=1)
    came = swap_z(term[:FIRST].astype(BF), 1).astype(F32)
    more = swap_z(term[FIRST:SECOND].astype(BF), -1).astype(F32)
    keep = term[SECOND:] + more
    hub_a, own, hub_b = keep[:PADDED], keep[PADDED:FIRST], keep[FIRST:]
    hub_a, own = hub_a + came[:PADDED], own + came[PADDED:]
    came = swap_z(hub_a.astype(BF), 3).astype(F32)
    own = own + swap_z(hub_b.astype(BF), -3).astype(F32) + came
    mine, other = own[:OWNED], own[OWNED:CHIP]
    came = swap_core(jnp.where(core == 0, other, mine))
    mine = jnp.where(core == 0, mine, other)
    grads = jnp.concatenate(
        [jnp.where(core == 0, mine, came), jnp.where(core == 0, came, mine)], axis=1
    )

    grads = (grads * scale)[None]
    new_first = 0.9 * first_moment + 0.1 * grads
    new_second = 0.999 * second_moment + 0.001 * grads * grads
    update = (
        new_first / (1.0 - 0.9**10) / (jnp.sqrt(new_second / (1.0 - 0.999**10)) + 1e-08)
    ).astype(BF)[0]

    around = [update] + [swap_y(update, m) for m in (1, 2, 3)]
    ordered = jnp.stack([lax.select_n(y ^ a, *around) for a in range(NY)])
    change = jnp.einsum("dr,acr->dac", basis[0], ordered, preferred_element_type=F32)
    return (new_first, new_second, change.astype(BF)[None])


def solution(mesh):
    return jax.shard_map(
        local,
        mesh=mesh,
        in_specs=(
            P(None, "dp", "tensor"),
            P(None, "dp", "tensor"),
            P(None, "tensor", None),
            P(None, ("tensor", "dp"), None),
            P(None, ("tensor", "dp"), None),
        ),
        out_specs=(
            P(None, ("tensor", "dp"), None),
            P(None, ("tensor", "dp"), None),
            P(None, "tensor", None, "dp"),
        ),
        check_vma=False,
    )
```

```python
import jax
import jax.numpy as jnp
from jax import lax
from jax.experimental import pallas as pl
from jax.experimental.layout import Layout, with_layout_constraint
from jax.experimental.pallas import tpu as pltpu
from jax.sharding import PartitionSpec as P

NX, NZ, NCORE, NY = 4, 8, 2, 4
OWNED = 43
CHUNKS = 2
CHIP, PADDED = NCORE * OWNED, 88
BF, F32 = jnp.bfloat16, jnp.float32

Z_ORDER = (-2, 1, -4, -1, 2, 3, 0, -3)
FIRST, SECOND = 2 * PADDED, 5 * PADDED
X_ORDER = (1, 2, 3, 0)
Y_PAIRS = ((1, 3), (3, 1))


def send(value, move):
    pairs = []
    for d in range(NX * NZ * NCORE * NY):
        x, z, c, y = d // (NZ * NCORE * NY), d // (NCORE * NY) % NZ, d // NY % NCORE, d % NY
        x, z, c, y = move(x, z, c, y)
        pairs.append((d, ((x * NZ + z) * NCORE + c) * NY + y))
    value = with_layout_constraint(value, Layout(major_to_minor=(0, 1)))
    return lax.ppermute(value, ("dp", "tensor"), pairs)


def swap_core(value):
    return send(value, lambda x, z, c, y: (x, z, 1 - c, y))


def swap_x(value, m):
    return send(value, lambda x, z, c, y: (x ^ m, z, c, y))


def swap_z(value, k):
    return send(value, lambda x, z, c, y: (x, (z + k * (1 - 2 * (z % 2))) % NZ, c, y))


def swap_y(value, m):
    return send(value, lambda x, z, c, y: (x, z, c, y ^ m))


def arrange_kernel(order_ref, own, came, *refs):
    outs, blocks = refs[:-1], refs[-1]
    rows, tokens = own.shape
    for s, source in enumerate((own, came)):
        for n in range(NX * NZ):
            start = n * CHIP
            low = start // 16 * 16
            high = min(rows, -(-(start + PADDED) // 16) * 16)
            piece = source[low:high, :].astype(F32)
            piece = piece[start - low : min(start - low + PADDED, high - low), :]
            if piece.shape[0] < PADDED:
                fill = jnp.zeros((PADDED - piece.shape[0], tokens), F32)
                piece = jnp.concatenate([piece, fill], axis=0)
            blocks[n, :, s * tokens : (s + 1) * tokens] = piece
    k = 0
    for out in outs:
        for i in range(0, out.shape[0], 2 * PADDED):
            pair = [blocks[order_ref[k + j]] for j in range(2)]
            out[i : i + 2 * PADDED, :] = jnp.concatenate(pair, axis=0).astype(BF)
            k += 2


def arrange(order, own, came):
    tokens = own.shape[1]
    sizes = [NZ * PADDED] * NX + [NX * n for n in (FIRST, SECOND - FIRST, SECOND - FIRST)]
    vmem = pl.BlockSpec(memory_space=pltpu.VMEM)
    smem = pl.BlockSpec(memory_space=pltpu.SMEM)
    return pl.pallas_call(
        arrange_kernel,
        out_shape=[jax.ShapeDtypeStruct((n, NCORE * tokens), BF) for n in sizes],
        in_specs=[smem, vmem, vmem],
        out_specs=[vmem] * len(sizes),
        scratch_shapes=[pltpu.VMEM((NX * NZ, PADDED, NCORE * tokens), F32)],
        compiler_params=pltpu.CompilerParams(vmem_limit_bytes=20 * 1024 * 1024),
        cost_estimate=pl.CostEstimate(flops=0, bytes_accessed=8 * 1024 * 1024, transcendentals=0),
    )(order, own, came)


def dot(a, b):
    out = lax.dot_general(a, b, (((1,), (0,)), ((), ())), preferred_element_type=F32)
    return with_layout_constraint(out, Layout(major_to_minor=(0, 1)))


def local(features, cotangent, basis, first_moment, second_moment):
    lanes = basis.shape[2] // NCORE
    scale = 1.0 / (features.shape[1] * lax.axis_size("dp"))
    dp = lax.axis_index("dp")
    core, z, x = dp & 1, (dp >> 1) & (NZ - 1), dp >> 4
    y = lax.axis_index("tensor")

    columns = cotangent[0].T
    other_columns = swap_core(columns)
    up = 1 - 2 * (z & 1)
    blocks_z = (z + up * jnp.array(Z_ORDER, jnp.int32)) & (NZ - 1)
    blocks_x = (x ^ jnp.array(X_ORDER, jnp.int32))[:, None] * NZ
    order = blocks_x + blocks_z[None, :]
    order = [order] + [order[:, i:j] for i, j in ((0, 2), (2, 5), (5, 8))]
    order = jnp.concatenate([part.reshape(-1) for part in order])

    def lanes_of(c):
        return lax.dynamic_slice(basis[0], (0, c * lanes), (basis.shape[1], lanes))

    theirs = swap_core(dot(features[0], lanes_of(1 - core)).astype(BF))
    partial = jnp.concatenate([dot(features[0], lanes_of(core)), theirs.astype(F32)], axis=0)
    width = lanes // CHUNKS
    chunks = [partial[:, c * width : (c + 1) * width] for c in range(CHUNKS)]
    chunks = [p + swap_y(p.astype(BF), m[0]).astype(F32) for p, m in zip(chunks, Y_PAIRS)]
    chunks, other_columns = lax.optimization_barrier((chunks, other_columns))
    parts = arrange(order, columns, other_columns)
    chunks = [p + swap_y(p.astype(BF), m[1]).astype(F32) for p, m in zip(chunks, Y_PAIRS)]
    chunks = [p.astype(BF) for p in chunks]
    chunks[0], parts = lax.optimization_barrier((chunks[0], parts))

    def send_x(sent):
        return [swap_x(value.astype(BF), m) for value, m in zip(sent, X_ORDER)]

    def send_z(first, second):
        return [swap_z(first.astype(BF), 1), swap_z(second.astype(BF), -1)]

    def add_x(keep, came):
        return keep + came[0].astype(F32) + came[1].astype(F32) + came[2].astype(F32)

    def add_z(keep, came):
        keep = (keep + came[1].astype(F32)).reshape(-1, SECOND - FIRST, width)
        first = came[0].astype(F32).reshape(-1, FIRST, width)
        return jnp.concatenate([keep[:, :FIRST] + first, keep[:, FIRST:]], axis=1)

    came_x = send_x([dot(part, chunks[0]) for part in parts[:3]])
    came_z = send_z(dot(parts[4], chunks[1]), dot(parts[5], chunks[1]))
    came_x, came_z = lax.optimization_barrier((came_x, came_z))
    a = add_x(dot(parts[3], chunks[0]), came_x)
    b = add_z(dot(parts[6], chunks[1]), came_z)
    came_z = send_z(a[:FIRST], a[FIRST:SECOND])
    came_x = send_x([b[0], b[1], b[2]])
    a = add_z(a[SECOND:], came_z)[0]
    b = add_x(b[3], came_x)
    keep = jnp.concatenate([a, b], axis=1)
    hub_a, own, hub_b = keep[:PADDED], keep[PADDED:FIRST], keep[FIRST:]
    came = swap_z(hub_a.astype(BF), 3).astype(F32)
    own = own + swap_z(hub_b.astype(BF), -3).astype(F32) + came
    mine, other = own[:OWNED], own[OWNED:CHIP]
    came = swap_core(jnp.where(core == 0, other, mine))
    mine = jnp.where(core == 0, mine, other)
    grads = jnp.concatenate(
        [jnp.where(core == 0, mine, came), jnp.where(core == 0, came, mine)], axis=1
    )

    grads = (grads * scale)[None]
    new_first = 0.9 * first_moment + 0.1 * grads
    new_second = 0.999 * second_moment + 0.001 * grads * grads
    update = (
        new_first / (1.0 - 0.9**10) / (jnp.sqrt(new_second / (1.0 - 0.999**10)) + 1e-08)
    ).astype(BF)[0]

    around = [update] + [swap_y(update, m) for m in (1, 2, 3)]
    ordered = jnp.stack([lax.select_n(y ^ a, *around) for a in range(NY)])
    change = jnp.einsum("dr,acr->dac", basis[0], ordered, preferred_element_type=F32)
    return (new_first, new_second, change.astype(BF)[None])


def solution(mesh):
    return jax.shard_map(
        local,
        mesh=mesh,
        in_specs=(
            P(None, "dp", "tensor"),
            P(None, "dp", "tensor"),
            P(None, "tensor", None),
            P(None, ("tensor", "dp"), None),
            P(None, ("tensor", "dp"), None),
        ),
        out_specs=(
            P(None, ("tensor", "dp"), None),
            P(None, ("tensor", "dp"), None),
            P(None, "tensor", None, "dp"),
        ),
        check_vma=False,
    )
```

```python
import jax
import jax.numpy as jnp
from jax import lax
from jax.experimental import pallas as pl
from jax.experimental.layout import Layout, with_layout_constraint
from jax.experimental.pallas import tpu as pltpu
from jax.sharding import PartitionSpec as P

NX, NZ, NCORE, NY = 4, 8, 2, 4
OWNED = 43
CHIP, PADDED = NCORE * OWNED, 88
BF, F32 = jnp.bfloat16, jnp.float32

Z_ORDER = (3, 1, -1, -3, -2, 0, 2, 4)
FIRST, SECOND, KEEP = 2 * PADDED, 4 * PADDED, 7 * PADDED
X_ORDER = (1, 2, 3, 0)


def send(value, move):
    pairs = []
    for d in range(NX * NZ * NCORE * NY):
        x, z, c, y = d // (NZ * NCORE * NY), d // (NCORE * NY) % NZ, d // NY % NCORE, d % NY
        x, z, c, y = move(x, z, c, y)
        pairs.append((d, ((x * NZ + z) * NCORE + c) * NY + y))
    value = with_layout_constraint(value, Layout(major_to_minor=(0, 1)))
    return lax.ppermute(value, ("dp", "tensor"), pairs)


def swap_core(value):
    return send(value, lambda x, z, c, y: (x, z, 1 - c, y))


def swap_x(value, m):
    return send(value, lambda x, z, c, y: (x ^ m, z, c, y))


def swap_z(value, k):
    return send(value, lambda x, z, c, y: (x, (z + k * (1 - 2 * (z % 2))) % NZ, c, y))


def swap_z2(value, shift):
    return send(value, lambda x, z, c, y: (x, ((z + shift) % NZ ^ 2) - shift & (NZ - 1), c, y))


def swap_y(value, m):
    return send(value, lambda x, z, c, y: (x, z, c, y ^ m))


def arrange_kernel(order_ref, own, came, *refs):
    outs, blocks = refs[:-1], refs[-1]
    rows, tokens = own.shape
    for s, source in enumerate((own, came)):
        for n in range(NX * NZ):
            start = n * CHIP
            low = start // 16 * 16
            high = min(rows, -(-(start + PADDED) // 16) * 16)
            piece = source[low:high, :].astype(F32)
            piece = piece[start - low : min(start - low + PADDED, high - low), :]
            if piece.shape[0] < PADDED:
                fill = jnp.zeros((PADDED - piece.shape[0], tokens), F32)
                piece = jnp.concatenate([piece, fill], axis=0)
            blocks[n, :, s * tokens : (s + 1) * tokens] = piece
    k = 0
    for out in outs:
        for i in range(0, out.shape[0], 2 * PADDED):
            pair = [blocks[order_ref[k + j]] for j in range(2)]
            out[i : i + 2 * PADDED, :] = jnp.concatenate(pair, axis=0).astype(BF)
            k += 2


def arrange(order, own, came):
    tokens = own.shape[1]
    sizes = [NZ * PADDED] * NX
    vmem = pl.BlockSpec(memory_space=pltpu.VMEM)
    smem = pl.BlockSpec(memory_space=pltpu.SMEM)
    return pl.pallas_call(
        arrange_kernel,
        out_shape=[jax.ShapeDtypeStruct((n, NCORE * tokens), BF) for n in sizes],
        in_specs=[smem, vmem, vmem],
        out_specs=[vmem] * len(sizes),
        scratch_shapes=[pltpu.VMEM((NX * NZ, PADDED, NCORE * tokens), F32)],
        compiler_params=pltpu.CompilerParams(vmem_limit_bytes=20 * 1024 * 1024),
        cost_estimate=pl.CostEstimate(flops=0, bytes_accessed=8 * 1024 * 1024, transcendentals=0),
    )(order, own, came)


def dot(a, b):
    out = lax.dot_general(a, b, (((1,), (0,)), ((), ())), preferred_element_type=F32)
    return with_layout_constraint(out, Layout(major_to_minor=(0, 1)))


def local(features, cotangent, basis, first_moment, second_moment):
    lanes = basis.shape[2] // NCORE
    scale = 1.0 / (features.shape[1] * lax.axis_size("dp"))
    dp = lax.axis_index("dp")
    core, z, x = dp & 1, (dp >> 1) & (NZ - 1), dp >> 4
    y = lax.axis_index("tensor")

    columns = cotangent[0].T
    other_columns = swap_core(columns)
    up = 1 - 2 * (z & 1)
    blocks_z = (z + up * jnp.array(Z_ORDER, jnp.int32)) & (NZ - 1)
    blocks_x = (x ^ jnp.array(X_ORDER, jnp.int32))[:, None] * NZ
    order = (blocks_x + blocks_z[None, :]).reshape(-1)

    def lanes_of(c):
        return lax.dynamic_slice(basis[0], (0, c * lanes), (basis.shape[1], lanes))

    theirs = swap_core(dot(features[0], lanes_of(1 - core)).astype(BF))
    partial = jnp.concatenate([dot(features[0], lanes_of(core)), theirs.astype(F32)], axis=0)
    sent = partial.astype(BF)
    came = [swap_y(sent, m) for m in (1, 2, 3)]
    came[0], other_columns = lax.optimization_barrier((came[0], other_columns))
    parts = arrange(order, columns, other_columns)
    came[2], parts = lax.optimization_barrier((came[2], parts))
    partial = partial + came[0].astype(F32) + came[1].astype(F32) + came[2].astype(F32)
    projected = partial.astype(BF)

    came = [swap_x(dot(part, projected).astype(BF), m) for part, m in zip(parts, X_ORDER[:3])]
    term = dot(parts[3], projected)
    term = term + came[0].astype(F32) + came[1].astype(F32) + came[2].astype(F32)
    lower, upper = swap_z(term[:FIRST].astype(BF), 1), swap_z(term[FIRST:SECOND].astype(BF), -1)
    opposite = swap_z(term[KEEP:].astype(BF), 4)
    keep = term[SECOND:KEEP]
    lower, upper = lower.astype(F32), upper.astype(F32)
    hub_a = keep[:PADDED] + lower[:PADDED]
    own = keep[PADDED:FIRST] + lower[PADDED:] + upper[:PADDED]
    hub_b = keep[FIRST:] + upper[PADDED:]
    straight = ((z ^ (z >> 1)) & 1) == 0
    near, far = jnp.where(straight, hub_b, hub_a), jnp.where(straight, hub_a, hub_b)
    near, far = swap_z2(near.astype(BF), 0), swap_z2(far.astype(BF), 2)
    own = own + near.astype(F32) + far.astype(F32) + opposite.astype(F32)
    mine, other = own[:OWNED], own[OWNED:CHIP]
    came = swap_core(jnp.where(core == 0, other, mine))
    mine = jnp.where(core == 0, mine, other)
    grads = jnp.concatenate(
        [jnp.where(core == 0, mine, came), jnp.where(core == 0, came, mine)], axis=1
    )

    grads = (grads * scale)[None]
    new_first = 0.9 * first_moment + 0.1 * grads
    new_second = 0.999 * second_moment + 0.001 * grads * grads
    update = (
        new_first / (1.0 - 0.9**10) / (jnp.sqrt(new_second / (1.0 - 0.999**10)) + 1e-08)
    ).astype(BF)[0]

    around = [update] + [swap_y(update, m) for m in (1, 2, 3)]
    ordered = jnp.stack([lax.select_n(y ^ a, *around) for a in range(NY)])
    change = jnp.einsum("dr,acr->dac", basis[0], ordered, preferred_element_type=F32)
    return (new_first, new_second, change.astype(BF)[None])


def solution(mesh):
    return jax.shard_map(
        local,
        mesh=mesh,
        in_specs=(
            P(None, "dp", "tensor"),
            P(None, "dp", "tensor"),
            P(None, "tensor", None),
            P(None, ("tensor", "dp"), None),
            P(None, ("tensor", "dp"), None),
        ),
        out_specs=(
            P(None, ("tensor", "dp"), None),
            P(None, ("tensor", "dp"), None),
            P(None, "tensor", None, "dp"),
        ),
        check_vma=False,
    )
```

```python
import jax
import jax.numpy as jnp
from jax import lax
from jax.experimental import pallas as pl
from jax.experimental.layout import Layout, with_layout_constraint
from jax.experimental.pallas import tpu as pltpu
from jax.sharding import PartitionSpec as P

NX, NZ, NCORE, NY = 4, 8, 2, 4
OWNED = 43
CHUNKS = 2
CHIP, PADDED = NCORE * OWNED, 88
BF, F32 = jnp.bfloat16, jnp.float32

Z_ORDER = (3, 1, -1, -3, -2, 0, 2, 4)
FIRST, SECOND, KEEP = 2 * PADDED, 4 * PADDED, 7 * PADDED
X_ORDER = ((2, 1, 3, 0), (2, 3, 1, 0))
PAIRS = ((1, 3), (3, 1))


def send(value, move):
    pairs = []
    for d in range(NX * NZ * NCORE * NY):
        x, z, c, y = d // (NZ * NCORE * NY), d // (NCORE * NY) % NZ, d // NY % NCORE, d % NY
        x, z, c, y = move(x, z, c, y)
        pairs.append((d, ((x * NZ + z) * NCORE + c) * NY + y))
    value = with_layout_constraint(value, Layout(major_to_minor=(0, 1)))
    return lax.ppermute(value, ("dp", "tensor"), pairs)


def swap_core(value):
    return send(value, lambda x, z, c, y: (x, z, 1 - c, y))


def swap_x(value, m):
    return send(value, lambda x, z, c, y: (x ^ m, z, c, y))


def swap_z(value, k):
    return send(value, lambda x, z, c, y: (x, (z + k * (1 - 2 * (z % 2))) % NZ, c, y))


def swap_z2(value, shift):
    return send(value, lambda x, z, c, y: (x, ((z + shift) % NZ ^ 2) - shift & (NZ - 1), c, y))


def swap_y(value, m):
    return send(value, lambda x, z, c, y: (x, z, c, y ^ m))


def arrange_kernel(order_ref, own, came, *refs):
    outs, blocks = refs[:-1], refs[-1]
    rows, tokens = own.shape
    for s, source in enumerate((own, came)):
        for n in range(NX * NZ):
            start = n * CHIP
            low = start // 16 * 16
            high = min(rows, -(-(start + PADDED) // 16) * 16)
            piece = source[low:high, :].astype(F32)
            piece = piece[start - low : min(start - low + PADDED, high - low), :]
            if piece.shape[0] < PADDED:
                fill = jnp.zeros((PADDED - piece.shape[0], tokens), F32)
                piece = jnp.concatenate([piece, fill], axis=0)
            blocks[n, :, s * tokens : (s + 1) * tokens] = piece
    half = NX * NZ // 2
    for k, out in enumerate(outs):
        for i in range(0, half, 2):
            pair = [blocks[order_ref[k * half + i + j]] for j in range(2)]
            out[i * PADDED : (i + 2) * PADDED, :] = jnp.concatenate(pair, axis=0).astype(BF)


def arrange(order, own, came):
    tokens = own.shape[1]
    shape = jax.ShapeDtypeStruct((NX * NZ // 2 * PADDED, NCORE * tokens), BF)
    vmem = pl.BlockSpec(memory_space=pltpu.VMEM)
    smem = pl.BlockSpec(memory_space=pltpu.SMEM)
    return pl.pallas_call(
        arrange_kernel,
        out_shape=[shape] * 2 * CHUNKS,
        in_specs=[smem, vmem, vmem],
        out_specs=[vmem] * 2 * CHUNKS,
        scratch_shapes=[pltpu.VMEM((NX * NZ, PADDED, NCORE * tokens), F32)],
        compiler_params=pltpu.CompilerParams(vmem_limit_bytes=20 * 1024 * 1024),
        cost_estimate=pl.CostEstimate(flops=0, bytes_accessed=8 * 1024 * 1024, transcendentals=0),
    )(order, own, came)


def dot(a, b):
    out = lax.dot_general(a, b, (((1,), (0,)), ((), ())), preferred_element_type=F32)
    return with_layout_constraint(out, Layout(major_to_minor=(0, 1)))


def local(features, cotangent, basis, first_moment, second_moment):
    lanes = basis.shape[2] // NCORE
    scale = 1.0 / (features.shape[1] * lax.axis_size("dp"))
    dp = lax.axis_index("dp")
    core, z, x = dp & 1, (dp >> 1) & (NZ - 1), dp >> 4
    y = lax.axis_index("tensor")

    columns = cotangent[0].T
    other_columns = swap_core(columns)
    up = 1 - 2 * (z & 1)
    blocks_z = (z + up * jnp.array(Z_ORDER, jnp.int32)) & (NZ - 1)
    blocks_x = x ^ jnp.array(X_ORDER, jnp.int32).reshape(-1)
    order = (blocks_x[:, None] * NZ + blocks_z[None, :]).reshape(-1)

    def lanes_of(c):
        return lax.dynamic_slice(basis[0], (0, c * lanes), (basis.shape[1], lanes))

    theirs = swap_core(dot(features[0], lanes_of(1 - core)).astype(BF))
    partial = jnp.concatenate([dot(features[0], lanes_of(core)), theirs.astype(F32)], axis=0)
    width = lanes // CHUNKS
    chunks = [partial[:, c * width : (c + 1) * width] for c in range(CHUNKS)]
    chunks = [p + swap_y(p.astype(BF), m[0]).astype(F32) for p, m in zip(chunks, PAIRS)]
    chunks, other_columns = lax.optimization_barrier((chunks, other_columns))
    parts = arrange(order, columns, other_columns)
    chunks = [p + swap_y(p.astype(BF), m[1]).astype(F32) for p, m in zip(chunks, PAIRS)]
    chunks = [p.astype(BF) for p in chunks]
    chunks[0], parts = lax.optimization_barrier((chunks[0], parts))

    rows = NZ * PADDED
    sent = [dot(parts[2 * c], p).astype(BF) for c, p in enumerate(chunks)]
    came = [swap_x(value, m[0]) for value, m in zip(sent, PAIRS)]
    chunks, sent = lax.optimization_barrier((chunks, sent))
    kept = [dot(parts[2 * c + 1], p) for c, p in enumerate(chunks)]
    terms = [k + c.astype(F32) for k, c in zip(lax.optimization_barrier(kept), came)]
    came = [swap_x(t[:rows].astype(BF), m[1]) for t, m in zip(terms, PAIRS)]
    terms = [t[rows:] + c.astype(F32) for t, c in zip(terms, came)]
    term = jnp.concatenate(terms, axis=1)
    lower, upper = swap_z(term[:FIRST].astype(BF), 1), swap_z(term[FIRST:SECOND].astype(BF), -1)
    opposite = swap_z(term[KEEP:].astype(BF), 4)
    keep = term[SECOND:KEEP]
    lower, upper = lower.astype(F32), upper.astype(F32)
    hub_a = keep[:PADDED] + lower[:PADDED]
    own = keep[PADDED:FIRST] + lower[PADDED:] + upper[:PADDED]
    hub_b = keep[FIRST:] + upper[PADDED:]
    straight = ((z ^ (z >> 1)) & 1) == 0
    near, far = jnp.where(straight, hub_b, hub_a), jnp.where(straight, hub_a, hub_b)
    near, far = swap_z2(near.astype(BF), 0), swap_z2(far.astype(BF), 2)
    own = own + near.astype(F32) + far.astype(F32) + opposite.astype(F32)
    mine, other = own[:OWNED], own[OWNED:CHIP]
    came = swap_core(jnp.where(core == 0, other, mine))
    mine = jnp.where(core == 0, mine, other)
    grads = jnp.concatenate(
        [jnp.where(core == 0, mine, came), jnp.where(core == 0, came, mine)], axis=1
    )

    grads = (grads * scale)[None]
    new_first = 0.9 * first_moment + 0.1 * grads
    new_second = 0.999 * second_moment + 0.001 * grads * grads
    update = (
        new_first / (1.0 - 0.9**10) / (jnp.sqrt(new_second / (1.0 - 0.999**10)) + 1e-08)
    ).astype(BF)[0]

    around = [update] + [swap_y(update, m) for m in (1, 2, 3)]
    ordered = jnp.stack([lax.select_n(y ^ a, *around) for a in range(NY)], axis=1)
    rows = lax.optimization_barrier(ordered.reshape(-1, ordered.shape[2]))
    change = dot(rows, basis[0].T).reshape(OWNED, NY, -1)
    return (new_first, new_second, change.astype(BF).transpose(2, 1, 0)[None])


def solution(mesh):
    return jax.shard_map(
        local,
        mesh=mesh,
        in_specs=(
            P(None, "dp", "tensor"),
            P(None, "dp", "tensor"),
            P(None, "tensor", None),
            P(None, ("tensor", "dp"), None),
            P(None, ("tensor", "dp"), None),
        ),
        out_specs=(
            P(None, ("tensor", "dp"), None),
            P(None, ("tensor", "dp"), None),
            P(None, "tensor", None, "dp"),
        ),
        check_vma=False,
    )
```

```python
import jax
import jax.numpy as jnp
from jax import lax
from jax.experimental import pallas as pl
from jax.experimental.layout import Layout, with_layout_constraint
from jax.experimental.pallas import tpu as pltpu
from jax.sharding import PartitionSpec as P

NX, NZ, NCORE, NY = 4, 8, 2, 4
OWNED = 43
CHUNKS, PIECES = 2, 4
CHIP, PADDED = NCORE * OWNED, 88
BF, F32 = jnp.bfloat16, jnp.float32

Z_ORDER = (3, 1, -1, -3, -2, 0, 2, 4)
FIRST, SECOND, KEEP = 2 * PADDED, 4 * PADDED, 7 * PADDED
X_ORDER = ((2, 1, 3, 0), (2, 3, 1, 0))
PAIRS = ((1, 3), (3, 1))


def send(value, move):
    pairs = []
    for d in range(NX * NZ * NCORE * NY):
        x, z, c, y = d // (NZ * NCORE * NY), d // (NCORE * NY) % NZ, d // NY % NCORE, d % NY
        x, z, c, y = move(x, z, c, y)
        pairs.append((d, ((x * NZ + z) * NCORE + c) * NY + y))
    value = with_layout_constraint(value, Layout(major_to_minor=(0, 1)))
    return lax.ppermute(value, ("dp", "tensor"), pairs)


def swap_core(value):
    return send(value, lambda x, z, c, y: (x, z, 1 - c, y))


def swap_x(value, m):
    return send(value, lambda x, z, c, y: (x ^ m, z, c, y))


def swap_z(value, k):
    return send(value, lambda x, z, c, y: (x, (z + k * (1 - 2 * (z % 2))) % NZ, c, y))


def swap_z2(value, shift):
    return send(value, lambda x, z, c, y: (x, ((z + shift) % NZ ^ 2) - shift & (NZ - 1), c, y))


def swap_y(value, m):
    return send(value, lambda x, z, c, y: (x, z, c, y ^ m))


def arrange_kernel(order_ref, own, came, *refs):
    outs, blocks = refs[:-1], refs[-1]
    rows, tokens = own.shape
    for s, source in enumerate((own, came)):
        for n in range(NX * NZ):
            start = n * CHIP
            low = start // 16 * 16
            high = min(rows, -(-(start + PADDED) // 16) * 16)
            piece = source[low:high, :].astype(F32)
            piece = piece[start - low : min(start - low + PADDED, high - low), :]
            if piece.shape[0] < PADDED:
                fill = jnp.zeros((PADDED - piece.shape[0], tokens), F32)
                piece = jnp.concatenate([piece, fill], axis=0)
            blocks[n, :, s * tokens : (s + 1) * tokens] = piece
    half = NX * NZ // 2
    for k, out in enumerate(outs):
        for i in range(0, half, 2):
            pair = [blocks[order_ref[k * half + i + j]] for j in range(2)]
            out[i * PADDED : (i + 2) * PADDED, :] = jnp.concatenate(pair, axis=0).astype(BF)


def arrange(order, own, came):
    tokens = own.shape[1]
    shape = jax.ShapeDtypeStruct((NX * NZ // 2 * PADDED, NCORE * tokens), BF)
    vmem = pl.BlockSpec(memory_space=pltpu.VMEM)
    smem = pl.BlockSpec(memory_space=pltpu.SMEM)
    return pl.pallas_call(
        arrange_kernel,
        out_shape=[shape] * 2 * CHUNKS,
        in_specs=[smem, vmem, vmem],
        out_specs=[vmem] * 2 * CHUNKS,
        scratch_shapes=[pltpu.VMEM((NX * NZ, PADDED, NCORE * tokens), F32)],
        compiler_params=pltpu.CompilerParams(vmem_limit_bytes=20 * 1024 * 1024),
        cost_estimate=pl.CostEstimate(flops=0, bytes_accessed=8 * 1024 * 1024, transcendentals=0),
    )(order, own, came)


def project_kernel(core_ref, features, basis, own, theirs, f_buf, b_buf, total, sems):
    pieces, tokens, depth = f_buf.shape
    lanes = own.shape[1]
    copies = []
    for k in range(pieces):
        part = pl.ds(k * depth, depth)
        copies.append(pltpu.make_async_copy(features.at[:, part], f_buf.at[k], sems.at[0, k]))
        copies.append(pltpu.make_async_copy(basis.at[part, :], b_buf.at[k], sems.at[1, k]))
    for copy in copies:
        copy.start()
    for k in range(pieces):
        copies[2 * k].wait()
        copies[2 * k + 1].wait()
        term = jnp.dot(f_buf[k], b_buf[k], preferred_element_type=F32)
        total[...] = term if k == 0 else total[...] + term
    for core in range(NCORE):

        @pl.when(core_ref[0] == core)
        def _(core=core):
            own[...] = total[:, core * lanes : (core + 1) * lanes]
            theirs[...] = total[:, (1 - core) * lanes : (2 - core) * lanes].astype(BF)


def project(core, features, basis):
    tokens, depth = features.shape
    rank = basis.shape[1]
    step = depth // PIECES
    vmem = pl.BlockSpec(memory_space=pltpu.VMEM)
    hbm = pl.BlockSpec(memory_space=pltpu.HBM)
    return pl.pallas_call(
        project_kernel,
        out_shape=[
            jax.ShapeDtypeStruct((tokens, rank // NCORE), F32),
            jax.ShapeDtypeStruct((tokens, rank // NCORE), BF),
        ],
        in_specs=[pl.BlockSpec(memory_space=pltpu.SMEM), hbm, hbm],
        out_specs=[vmem] * 2,
        scratch_shapes=[
            pltpu.VMEM((PIECES, tokens, step), BF),
            pltpu.VMEM((PIECES, step, rank), BF),
            pltpu.VMEM((tokens, rank), F32),
            pltpu.SemaphoreType.DMA((2, PIECES)),
        ],
        compiler_params=pltpu.CompilerParams(vmem_limit_bytes=8 * 1024 * 1024),
        cost_estimate=pl.CostEstimate(
            flops=2 * tokens * depth * rank, bytes_accessed=3 * 1024 * 1024, transcendentals=0
        ),
    )(core, features, basis)


def dot(a, b):
    out = lax.dot_general(a, b, (((1,), (0,)), ((), ())), preferred_element_type=F32)
    return with_layout_constraint(out, Layout(major_to_minor=(0, 1)))


def local(features, cotangent, basis, first_moment, second_moment):
    lanes = basis.shape[2] // NCORE
    scale = 1.0 / (features.shape[1] * lax.axis_size("dp"))
    dp = lax.axis_index("dp")
    core, z, x = dp & 1, (dp >> 1) & (NZ - 1), dp >> 4
    y = lax.axis_index("tensor")

    columns = cotangent[0].T
    other_columns = swap_core(columns)
    up = 1 - 2 * (z & 1)
    blocks_z = (z + up * jnp.array(Z_ORDER, jnp.int32)) & (NZ - 1)
    blocks_x = x ^ jnp.array(X_ORDER, jnp.int32).reshape(-1)
    order = (blocks_x[:, None] * NZ + blocks_z[None, :]).reshape(-1)

    own, theirs = project(core.reshape(1), features[0], basis[0])
    partial = jnp.concatenate([own, swap_core(theirs).astype(F32)], axis=0)
    width = lanes // CHUNKS
    chunks = [partial[:, c * width : (c + 1) * width] for c in range(CHUNKS)]
    chunks = [p + swap_y(p.astype(BF), m[0]).astype(F32) for p, m in zip(chunks, PAIRS)]
    chunks, other_columns = lax.optimization_barrier((chunks, other_columns))
    parts = arrange(order, columns, other_columns)
    chunks = [p + swap_y(p.astype(BF), m[1]).astype(F32) for p, m in zip(chunks, PAIRS)]
    chunks = [p.astype(BF) for p in chunks]
    chunks[0], parts = lax.optimization_barrier((chunks[0], parts))

    rows = NZ * PADDED
    sent = [dot(parts[2 * c], p).astype(BF) for c, p in enumerate(chunks)]
    came = [swap_x(value, m[0]) for value, m in zip(sent, PAIRS)]
    chunks, sent = lax.optimization_barrier((chunks, sent))
    kept = [dot(parts[2 * c + 1], p) for c, p in enumerate(chunks)]
    terms = [k + c.astype(F32) for k, c in zip(lax.optimization_barrier(kept), came)]
    came = [swap_x(t[:rows].astype(BF), m[1]) for t, m in zip(terms, PAIRS)]
    terms = [t[rows:] + c.astype(F32) for t, c in zip(terms, came)]
    term = jnp.concatenate(terms, axis=1)
    lower, upper = swap_z(term[:FIRST].astype(BF), 1), swap_z(term[FIRST:SECOND].astype(BF), -1)
    opposite = swap_z(term[KEEP:].astype(BF), 4)
    keep = term[SECOND:KEEP]
    lower, upper = lower.astype(F32), upper.astype(F32)
    hub_a = keep[:PADDED] + lower[:PADDED]
    own = keep[PADDED:FIRST] + lower[PADDED:] + upper[:PADDED]
    hub_b = keep[FIRST:] + upper[PADDED:]
    straight = ((z ^ (z >> 1)) & 1) == 0
    near, far = jnp.where(straight, hub_b, hub_a), jnp.where(straight, hub_a, hub_b)
    near, far = swap_z2(near.astype(BF), 0), swap_z2(far.astype(BF), 2)
    own = own + near.astype(F32) + far.astype(F32) + opposite.astype(F32)
    mine, other = own[:OWNED], own[OWNED:CHIP]
    came = swap_core(jnp.where(core == 0, other, mine))
    mine = jnp.where(core == 0, mine, other)
    grads = jnp.concatenate(
        [jnp.where(core == 0, mine, came), jnp.where(core == 0, came, mine)], axis=1
    )

    grads = (grads * scale)[None]
    new_first = 0.9 * first_moment + 0.1 * grads
    new_second = 0.999 * second_moment + 0.001 * grads * grads
    update = (
        new_first / (1.0 - 0.9**10) / (jnp.sqrt(new_second / (1.0 - 0.999**10)) + 1e-08)
    ).astype(BF)[0]

    around = [update]
    for m, more in ((1, 0), (2, 5), (3, 21)):
        around.append(swap_y(jnp.pad(update, ((0, more), (0, 0))), m)[:OWNED])
    ordered = jnp.stack([lax.select_n(y ^ a, *around) for a in range(NY)], axis=1)
    rows = lax.optimization_barrier(ordered.reshape(-1, ordered.shape[2]))
    change = dot(rows, basis[0].T).reshape(OWNED, NY, -1)
    return (new_first, new_second, change.astype(BF).transpose(2, 1, 0)[None])


def solution(mesh):
    return jax.shard_map(
        local,
        mesh=mesh,
        in_specs=(
            P(None, "dp", "tensor"),
            P(None, "dp", "tensor"),
            P(None, "tensor", None),
            P(None, ("tensor", "dp"), None),
            P(None, ("tensor", "dp"), None),
        ),
        out_specs=(
            P(None, ("tensor", "dp"), None),
            P(None, ("tensor", "dp"), None),
            P(None, "tensor", None, "dp"),
        ),
        check_vma=False,
    )
```

```python
import jax
import jax.numpy as jnp
from jax import lax
from jax.experimental import pallas as pl
from jax.experimental.layout import Layout, with_layout_constraint
from jax.experimental.pallas import tpu as pltpu
from jax.sharding import PartitionSpec as P

NX, NZ, NCORE, NY = 4, 8, 2, 4
OWNED = 43
CHIP, PADDED = NCORE * OWNED, 88
BF, F32 = jnp.bfloat16, jnp.float32

Z_ORDER = (3, 1, -1, -3, -2, 0, 2, 4)
FIRST, HALF = 2 * PADDED, 4 * PADDED
X_ORDER = ((2, 1, 3, 0), (2, 3, 1, 0))
PAIRS = ((1, 3), (3, 1))


def send(value, move):
    pairs = []
    for d in range(NX * NZ * NCORE * NY):
        x, z, c, y = d // (NZ * NCORE * NY), d // (NCORE * NY) % NZ, d // NY % NCORE, d % NY
        x, z, c, y = move(x, z, c, y)
        pairs.append((d, ((x * NZ + z) * NCORE + c) * NY + y))
    value = with_layout_constraint(value, Layout(major_to_minor=(0, 1)))
    return lax.ppermute(value, ("dp", "tensor"), pairs)


def swap_core(value):
    return send(value, lambda x, z, c, y: (x, z, 1 - c, y))


def swap_x(value, m):
    return send(value, lambda x, z, c, y: (x ^ m, z, c, y))


def swap_z(value, k):
    return send(value, lambda x, z, c, y: (x, (z + k * (1 - 2 * (z % 2))) % NZ, c, y))


def swap_z2(value, shift):
    return send(value, lambda x, z, c, y: (x, ((z + shift) % NZ ^ 2) - shift & (NZ - 1), c, y))


def swap_y(value, m):
    return send(value, lambda x, z, c, y: (x, z, c, y ^ m))


def arrange_kernel(order_ref, own, came, *refs):
    outs, blocks = refs[:-1], refs[-1]
    rows, tokens = own.shape
    for s, source in enumerate((own, came)):
        for n in range(NX * NZ):
            start = n * CHIP
            low = start // 16 * 16
            high = min(rows, -(-(start + PADDED) // 16) * 16)
            piece = source[low:high, :].astype(F32)
            piece = piece[start - low : min(start - low + PADDED, high - low), :]
            if piece.shape[0] < PADDED:
                fill = jnp.zeros((PADDED - piece.shape[0], tokens), F32)
                piece = jnp.concatenate([piece, fill], axis=0)
            blocks[n, :, s * tokens : (s + 1) * tokens] = piece
    k = 0
    for out in outs:
        for i in range(0, out.shape[0], 2 * PADDED):
            pair = [blocks[order_ref[k + j]] for j in range(2)]
            out[i : i + 2 * PADDED, :] = jnp.concatenate(pair, axis=0).astype(BF)
            k += 2


def arrange(order, own, came):
    tokens = own.shape[1]
    shape = jax.ShapeDtypeStruct((2 * HALF, NCORE * tokens), BF)
    vmem = pl.BlockSpec(memory_space=pltpu.VMEM)
    smem = pl.BlockSpec(memory_space=pltpu.SMEM)
    return pl.pallas_call(
        arrange_kernel,
        out_shape=[shape] * 4,
        in_specs=[smem, vmem, vmem],
        out_specs=[vmem] * 4,
        scratch_shapes=[pltpu.VMEM((NX * NZ, PADDED, NCORE * tokens), F32)],
        compiler_params=pltpu.CompilerParams(vmem_limit_bytes=20 * 1024 * 1024),
        cost_estimate=pl.CostEstimate(flops=0, bytes_accessed=8 * 1024 * 1024, transcendentals=0),
    )(order, own, came)


def dot(a, b):
    out = lax.dot_general(a, b, (((1,), (0,)), ((), ())), preferred_element_type=F32)
    return with_layout_constraint(out, Layout(major_to_minor=(0, 1)))


def local(features, cotangent, basis, first_moment, second_moment):
    lanes = basis.shape[2] // NCORE
    scale = 1.0 / (features.shape[1] * lax.axis_size("dp"))
    dp = lax.axis_index("dp")
    core, z, x = dp & 1, (dp >> 1) & (NZ - 1), dp >> 4
    y = lax.axis_index("tensor")

    up = 1 - 2 * (z & 1)
    blocks_z = (z + up * jnp.array(Z_ORDER, jnp.int32)) & (NZ - 1)
    blocks_z = blocks_z.reshape(2, 1, NZ // 2)
    blocks_x = (x ^ jnp.array(X_ORDER, jnp.int32)) * NZ
    order = (blocks_x[:, :, None] + blocks_z).reshape(-1)

    def lanes_of(c):
        return lax.dynamic_slice(basis[0], (0, c * lanes), (basis.shape[1], lanes))

    theirs = dot(features[0], lanes_of(1 - core)).astype(BF)
    columns = cotangent[0].T
    theirs, sent = lax.optimization_barrier((theirs, columns))
    other_columns = swap_core(sent)
    chunks = [dot(features[0], lanes_of(core)), swap_core(theirs).astype(F32)]
    chunks = [p + swap_y(p.astype(BF), m[0]).astype(F32) for p, m in zip(chunks, PAIRS)]
    chunks, other_columns = lax.optimization_barrier((chunks, other_columns))
    parts = arrange(order, columns, other_columns)
    chunks = [p + swap_y(p.astype(BF), m[1]).astype(F32) for p, m in zip(chunks, PAIRS)]
    projected = jnp.concatenate([p.astype(BF) for p in chunks], axis=0)
    projected, parts = lax.optimization_barrier((projected, parts))

    sent = [dot(part, projected).astype(BF) for part in parts[::2]]
    came = [swap_x(value, m[0]) for value, m in zip(sent, PAIRS)]
    projected, sent = lax.optimization_barrier((projected, sent))
    kept = lax.optimization_barrier([dot(part, projected) for part in parts[1::2]])
    kept = [k + c.astype(F32) for k, c in zip(kept, came)]
    came = [swap_x(k[:HALF].astype(BF), m[1]) for k, m in zip(kept, PAIRS)]
    leave, keep = [k[HALF:] + c.astype(F32) for k, c in zip(kept, came)]
    lower, upper = swap_z(leave[:FIRST].astype(BF), 1), swap_z(leave[FIRST:].astype(BF), -1)
    opposite = swap_z(keep[3 * PADDED :].astype(BF), 4)
    lower, upper = lower.astype(F32), upper.astype(F32)
    hub_a = keep[:PADDED] + lower[:PADDED]
    own = keep[PADDED:FIRST] + lower[PADDED:] + upper[:PADDED]
    hub_b = keep[FIRST : 3 * PADDED] + upper[PADDED:]
    straight = ((z ^ (z >> 1)) & 1) == 0
    near, far = jnp.where(straight, hub_b, hub_a), jnp.where(straight, hub_a, hub_b)
    near, far = swap_z2(near.astype(BF), 0), swap_z2(far.astype(BF), 2)
    own = own + near.astype(F32) + far.astype(F32) + opposite.astype(F32)
    mine, other = own[:OWNED], own[OWNED:CHIP]
    came = swap_core(jnp.where(core == 0, other, mine))
    mine = jnp.where(core == 0, mine, other)
    grads = jnp.concatenate(
        [jnp.where(core == 0, mine, came), jnp.where(core == 0, came, mine)], axis=1
    )

    grads = (grads * scale)[None]
    new_first = 0.9 * first_moment + 0.1 * grads
    new_second = 0.999 * second_moment + 0.001 * grads * grads
    update = (
        new_first / (1.0 - 0.9**10) / (jnp.sqrt(new_second / (1.0 - 0.999**10)) + 1e-08)
    ).astype(BF)[0]

    around = [update]
    for m, more in ((1, 0), (2, 5), (3, 21)):
        around.append(swap_y(jnp.pad(update, ((0, more), (0, 0))), m)[:OWNED])
    ordered = jnp.stack([lax.select_n(y ^ a, *around) for a in range(NY)], axis=1)
    rows = lax.optimization_barrier(ordered.reshape(-1, ordered.shape[2]))
    change = dot(rows, basis[0].T).reshape(OWNED, NY, -1)
    return (new_first, new_second, change.astype(BF).transpose(2, 1, 0)[None])


def solution(mesh):
    return jax.shard_map(
        local,
        mesh=mesh,
        in_specs=(
            P(None, "dp", "tensor"),
            P(None, "dp", "tensor"),
            P(None, "tensor", None),
            P(None, ("tensor", "dp"), None),
            P(None, ("tensor", "dp"), None),
        ),
        out_specs=(
            P(None, ("tensor", "dp"), None),
            P(None, ("tensor", "dp"), None),
            P(None, "tensor", None, "dp"),
        ),
        check_vma=False,
    )
```

```python
import jax
import jax.numpy as jnp
from jax import lax
from jax.experimental import pallas as pl
from jax.experimental.layout import Layout, with_layout_constraint
from jax.experimental.pallas import tpu as pltpu
from jax.sharding import PartitionSpec as P

NX, NZ, NCORE, NY = 4, 8, 2, 4
OWNED = 43
CHIP, PADDED = NCORE * OWNED, 88
BF, F32 = jnp.bfloat16, jnp.float32

Z_ORDER = (3, 1, -1, -3, -2, 0, 2, 4)
FIRST, HALF = 2 * PADDED, 4 * PADDED
X_ORDER = ((2, 1, 3, 0), (2, 3, 1, 0))
PAIRS = ((1, 3), (3, 1))


def send(value, move):
    pairs = []
    for d in range(NX * NZ * NCORE * NY):
        x, z, c, y = d // (NZ * NCORE * NY), d // (NCORE * NY) % NZ, d // NY % NCORE, d % NY
        x, z, c, y = move(x, z, c, y)
        pairs.append((d, ((x * NZ + z) * NCORE + c) * NY + y))
    value = with_layout_constraint(value, Layout(major_to_minor=(0, 1)))
    return lax.ppermute(value, ("dp", "tensor"), pairs)


def swap_core(value):
    return send(value, lambda x, z, c, y: (x, z, 1 - c, y))


def swap_x(value, m):
    return send(value, lambda x, z, c, y: (x ^ m, z, c, y))


def swap_z(value, k):
    return send(value, lambda x, z, c, y: (x, (z + k * (1 - 2 * (z % 2))) % NZ, c, y))


def swap_z2(value, shift):
    return send(value, lambda x, z, c, y: (x, ((z + shift) % NZ ^ 2) - shift & (NZ - 1), c, y))


def swap_y(value, m):
    return send(value, lambda x, z, c, y: (x, z, c, y ^ m))


def arrange_kernel(order_ref, own, came, *refs):
    outs, blocks = refs[:-1], refs[-1]
    rows, tokens = own.shape
    for s, source in enumerate((own, came)):
        for n in range(NX * NZ):
            start = n * CHIP
            low = start // 16 * 16
            high = min(rows, -(-(start + PADDED) // 16) * 16)
            piece = source[low:high, :].astype(F32)
            piece = piece[start - low : min(start - low + PADDED, high - low), :]
            if piece.shape[0] < PADDED:
                fill = jnp.zeros((PADDED - piece.shape[0], tokens), F32)
                piece = jnp.concatenate([piece, fill], axis=0)
            blocks[n, :, s * tokens : (s + 1) * tokens] = piece
    k = 0
    for out in outs:
        for i in range(0, out.shape[0], 2 * PADDED):
            pair = [blocks[order_ref[k + j]] for j in range(2)]
            out[i : i + 2 * PADDED, :] = jnp.concatenate(pair, axis=0).astype(BF)
            k += 2


def arrange(order, own, came):
    tokens = own.shape[1]
    shape = jax.ShapeDtypeStruct((2 * HALF, NCORE * tokens), BF)
    vmem = pl.BlockSpec(memory_space=pltpu.VMEM)
    smem = pl.BlockSpec(memory_space=pltpu.SMEM)
    return pl.pallas_call(
        arrange_kernel,
        out_shape=[shape] * 4,
        in_specs=[smem, vmem, vmem],
        out_specs=[vmem] * 4,
        scratch_shapes=[pltpu.VMEM((NX * NZ, PADDED, NCORE * tokens), F32)],
        compiler_params=pltpu.CompilerParams(vmem_limit_bytes=20 * 1024 * 1024),
        cost_estimate=pl.CostEstimate(flops=0, bytes_accessed=8 * 1024 * 1024, transcendentals=0),
    )(order, own, came)


def project_kernel(core_ref, features, basis, own, own_sent, theirs):
    lanes = own.shape[1]
    total = jnp.dot(features[...], basis[...], preferred_element_type=F32)
    halves = total[:, :lanes], total[:, lanes:]
    for core in range(NCORE):

        @pl.when(core_ref[0] == core)
        def _(core=core):
            own[...] = halves[core]
            own_sent[...] = halves[core].astype(BF)
            theirs[...] = halves[1 - core].astype(BF)


def project(core, features, basis):
    shape = features.shape[0], basis.shape[1] // NCORE
    vmem = pl.BlockSpec(memory_space=pltpu.VMEM)
    return pl.pallas_call(
        project_kernel,
        out_shape=[jax.ShapeDtypeStruct(shape, dtype) for dtype in (F32, BF, BF)],
        in_specs=[pl.BlockSpec(memory_space=pltpu.SMEM), vmem, vmem],
        out_specs=[vmem] * 3,
        compiler_params=pltpu.CompilerParams(vmem_limit_bytes=8 * 1024 * 1024),
        cost_estimate=pl.CostEstimate(
            flops=2 * features.size * basis.shape[1], bytes_accessed=2 * 1024 * 1024, transcendentals=0
        ),
    )(core, features, basis)


def dot(a, b):
    out = lax.dot_general(a, b, (((1,), (0,)), ((), ())), preferred_element_type=F32)
    return with_layout_constraint(out, Layout(major_to_minor=(0, 1)))


def local(features, cotangent, basis, first_moment, second_moment):
    scale = 1.0 / (features.shape[1] * lax.axis_size("dp"))
    dp = lax.axis_index("dp")
    core, z, x = dp & 1, (dp >> 1) & (NZ - 1), dp >> 4
    y = lax.axis_index("tensor")

    up = 1 - 2 * (z & 1)
    blocks_z = (z + up * jnp.array(Z_ORDER, jnp.int32)) & (NZ - 1)
    blocks_z = blocks_z.reshape(2, 1, NZ // 2)
    blocks_x = (x ^ jnp.array(X_ORDER, jnp.int32)) * NZ
    order = (blocks_x[:, :, None] + blocks_z).reshape(-1)

    mine, mine_sent, theirs = project(core.reshape(1), features[0], basis[0])
    columns = cotangent[0].T
    theirs, sent = lax.optimization_barrier((swap_core(theirs), columns))
    other_columns = swap_core(sent)
    came = [swap_y(p, m[0]) for p, m in zip((mine_sent, theirs), PAIRS)]
    chunks = [p.astype(F32) + c.astype(F32) for p, c in zip((mine, theirs), came)]
    came = [swap_y(p.astype(BF), m[1]) for p, m in zip(chunks, PAIRS)]
    parts = arrange(order, columns, other_columns)
    came[1], parts = lax.optimization_barrier((came[1], parts))
    chunks = [p + c.astype(F32) for p, c in zip(chunks, came)]
    projected = jnp.concatenate([p.astype(BF) for p in chunks], axis=0)

    sent = [dot(part, projected).astype(BF) for part in parts[::2]]
    came = [swap_x(value, m[0]) for value, m in zip(sent, PAIRS)]
    projected, sent = lax.optimization_barrier((projected, sent))
    kept = lax.optimization_barrier([dot(part, projected) for part in parts[1::2]])
    kept = [k + c.astype(F32) for k, c in zip(kept, came)]
    came = [swap_x(k[:HALF].astype(BF), m[1]) for k, m in zip(kept, PAIRS)]
    leave, keep = [k[HALF:] + c.astype(F32) for k, c in zip(kept, came)]
    lower, upper = swap_z(leave[:FIRST].astype(BF), 1), swap_z(leave[FIRST:].astype(BF), -1)
    opposite = swap_z(keep[3 * PADDED :].astype(BF), 4)
    lower, upper = lower.astype(F32), upper.astype(F32)
    hub_a = keep[:PADDED] + lower[:PADDED]
    own = keep[PADDED:FIRST] + lower[PADDED:] + upper[:PADDED]
    hub_b = keep[FIRST : 3 * PADDED] + upper[PADDED:]
    straight = ((z ^ (z >> 1)) & 1) == 0
    near, far = jnp.where(straight, hub_b, hub_a), jnp.where(straight, hub_a, hub_b)
    near, far = swap_z2(near.astype(BF), 0), swap_z2(far.astype(BF), 2)
    own = own + near.astype(F32) + far.astype(F32) + opposite.astype(F32)
    mine, other = own[:OWNED], own[OWNED:CHIP]
    came = swap_core(jnp.where(core == 0, other, mine))
    mine = jnp.where(core == 0, mine, other)
    grads = jnp.concatenate(
        [jnp.where(core == 0, mine, came), jnp.where(core == 0, came, mine)], axis=1
    )

    grads = (grads * scale)[None]
    new_first = 0.9 * first_moment + 0.1 * grads
    new_second = 0.999 * second_moment + 0.001 * grads * grads
    update = (
        new_first / (1.0 - 0.9**10) / (jnp.sqrt(new_second / (1.0 - 0.999**10)) + 1e-08)
    ).astype(BF)[0]

    around = [update]
    for m, more in ((1, 0), (2, 5), (3, 21)):
        around.append(swap_y(jnp.pad(update, ((0, more), (0, 0))), m)[:OWNED])
    ordered = jnp.stack([lax.select_n(y ^ a, *around) for a in range(NY)], axis=1)
    rows = lax.optimization_barrier(ordered.reshape(-1, ordered.shape[2]))
    change = dot(rows, basis[0].T).reshape(OWNED, NY, -1)
    return (new_first, new_second, change.astype(BF).transpose(2, 1, 0)[None])


def solution(mesh):
    return jax.shard_map(
        local,
        mesh=mesh,
        in_specs=(
            P(None, "dp", "tensor"),
            P(None, "dp", "tensor"),
            P(None, "tensor", None),
            P(None, ("tensor", "dp"), None),
            P(None, ("tensor", "dp"), None),
        ),
        out_specs=(
            P(None, ("tensor", "dp"), None),
            P(None, ("tensor", "dp"), None),
            P(None, "tensor", None, "dp"),
        ),
        check_vma=False,
    )
```

```python
import jax
import jax.numpy as jnp
from jax import lax
from jax.experimental import pallas as pl
from jax.experimental.layout import Layout, with_layout_constraint
from jax.experimental.pallas import tpu as pltpu
from jax.sharding import PartitionSpec as P

NX, NZ, NCORE, NY = 4, 8, 2, 4
OWNED = 43
CHIP, PADDED = NCORE * OWNED, 88
BF, F32 = jnp.bfloat16, jnp.float32

Z_ORDER = (3, 1, -1, -3, -2, 0, 2, 4)
FIRST, HALF = 2 * PADDED, 4 * PADDED
X_ORDER = ((2, 1, 3, 0), (2, 3, 1, 0))
PAIRS = ((1, 3), (3, 1))


def send(value, move):
    pairs = []
    for d in range(NX * NZ * NCORE * NY):
        x, z, c, y = d // (NZ * NCORE * NY), d // (NCORE * NY) % NZ, d // NY % NCORE, d % NY
        x, z, c, y = move(x, z, c, y)
        pairs.append((d, ((x * NZ + z) * NCORE + c) * NY + y))
    value = with_layout_constraint(value, Layout(major_to_minor=(0, 1)))
    return lax.ppermute(value, ("dp", "tensor"), pairs)


def swap_core(value):
    return send(value, lambda x, z, c, y: (x, z, 1 - c, y))


def swap_x(value, m):
    return send(value, lambda x, z, c, y: (x ^ m, z, c, y))


def swap_z(value, k):
    return send(value, lambda x, z, c, y: (x, (z + k * (1 - 2 * (z % 2))) % NZ, c, y))


def swap_z2(value, shift):
    return send(value, lambda x, z, c, y: (x, ((z + shift) % NZ ^ 2) - shift & (NZ - 1), c, y))


def swap_y(value, m):
    return send(value, lambda x, z, c, y: (x, z, c, y ^ m))


def arrange_kernel(order_ref, own, came, *refs):
    outs, blocks = refs[:-1], refs[-1]
    rows, tokens = own.shape
    for s, source in enumerate((own, came)):
        for n in range(NX * NZ):
            start = n * CHIP
            low = start // 16 * 16
            high = min(rows, -(-(start + PADDED) // 16) * 16)
            piece = source[low:high, :].astype(F32)
            piece = piece[start - low : min(start - low + PADDED, high - low), :]
            if piece.shape[0] < PADDED:
                fill = jnp.zeros((PADDED - piece.shape[0], tokens), F32)
                piece = jnp.concatenate([piece, fill], axis=0)
            blocks[n, :, s * tokens : (s + 1) * tokens] = piece
    k = 0
    for out in outs:
        for i in range(0, out.shape[0], 2 * PADDED):
            pair = [blocks[order_ref[k + j]] for j in range(2)]
            out[i : i + 2 * PADDED, :] = jnp.concatenate(pair, axis=0).astype(BF)
            k += 2


def arrange(order, own, came):
    tokens = own.shape[1]
    shape = jax.ShapeDtypeStruct((2 * HALF, NCORE * tokens), BF)
    vmem = pl.BlockSpec(memory_space=pltpu.VMEM)
    smem = pl.BlockSpec(memory_space=pltpu.SMEM)
    return pl.pallas_call(
        arrange_kernel,
        out_shape=[shape] * 4,
        in_specs=[smem, vmem, vmem],
        out_specs=[vmem] * 4,
        scratch_shapes=[pltpu.VMEM((NX * NZ, PADDED, NCORE * tokens), F32)],
        compiler_params=pltpu.CompilerParams(vmem_limit_bytes=20 * 1024 * 1024),
        cost_estimate=pl.CostEstimate(flops=0, bytes_accessed=8 * 1024 * 1024, transcendentals=0),
    )(order, own, came)


def project_kernel(core_ref, features, basis, own, own_sent, theirs):
    lanes = own.shape[1]
    total = jnp.dot(features[...], basis[...], preferred_element_type=F32)
    halves = total[:, :lanes], total[:, lanes:]
    for core in range(NCORE):

        @pl.when(core_ref[0] == core)
        def _(core=core):
            own[...] = halves[core]
            own_sent[...] = halves[core].astype(BF)
            theirs[...] = halves[1 - core].astype(BF)


def project(core, features, basis):
    shape = features.shape[0], basis.shape[1] // NCORE
    vmem = pl.BlockSpec(memory_space=pltpu.VMEM)
    return pl.pallas_call(
        project_kernel,
        out_shape=[jax.ShapeDtypeStruct(shape, dtype) for dtype in (F32, BF, BF)],
        in_specs=[pl.BlockSpec(memory_space=pltpu.SMEM), vmem, vmem],
        out_specs=[vmem] * 3,
        compiler_params=pltpu.CompilerParams(vmem_limit_bytes=8 * 1024 * 1024),
        cost_estimate=pl.CostEstimate(
            flops=2 * features.size * basis.shape[1], bytes_accessed=2 * 1024 * 1024, transcendentals=0
        ),
    )(core, features, basis)


def dot(a, b):
    out = lax.dot_general(a, b, (((1,), (0,)), ((), ())), preferred_element_type=F32)
    return with_layout_constraint(out, Layout(major_to_minor=(0, 1)))


def local(features, cotangent, basis, first_moment, second_moment):
    scale = 1.0 / (features.shape[1] * lax.axis_size("dp"))
    dp = lax.axis_index("dp")
    core, z, x = dp & 1, (dp >> 1) & (NZ - 1), dp >> 4
    y = lax.axis_index("tensor")

    up = 1 - 2 * (z & 1)
    blocks_z = (z + up * jnp.array(Z_ORDER, jnp.int32)) & (NZ - 1)
    blocks_z = blocks_z.reshape(2, 1, NZ // 2)
    blocks_x = (x ^ jnp.array(X_ORDER, jnp.int32)) * NZ
    order = (blocks_x[:, :, None] + blocks_z).reshape(-1)

    mine, mine_sent, theirs = project(core.reshape(1), features[0], basis[0])
    columns = cotangent[0].T
    other_columns = swap_core(columns)
    theirs = swap_core(theirs)
    came = [swap_y(p, m[0]) for p, m in zip((mine_sent, theirs), PAIRS)]
    chunks = [p.astype(F32) + c.astype(F32) for p, c in zip((mine, theirs), came)]
    came = [swap_y(p.astype(BF), m[1]) for p, m in zip(chunks, PAIRS)]
    parts = arrange(order, columns, other_columns)
    came[1], parts = lax.optimization_barrier((came[1], parts))
    chunks = [p + c.astype(F32) for p, c in zip(chunks, came)]
    projected = jnp.concatenate([p.astype(BF) for p in chunks], axis=0)

    sent = [dot(part, projected).astype(BF) for part in parts[::2]]
    came = [swap_x(value, m[0]) for value, m in zip(sent, PAIRS)]
    projected, sent[1] = lax.optimization_barrier((projected, sent[1]))
    kept = lax.optimization_barrier([dot(part, projected) for part in parts[1::2]])
    kept = [k + c.astype(F32) for k, c in zip(kept, came)]
    came = [swap_x(k[:HALF].astype(BF), m[1]) for k, m in zip(kept, PAIRS)]
    leave, keep = [k[HALF:] + c.astype(F32) for k, c in zip(kept, came)]
    lower, upper = swap_z(leave[:FIRST].astype(BF), 1), swap_z(leave[FIRST:].astype(BF), -1)
    opposite = swap_z(keep[3 * PADDED :].astype(BF), 4)
    lower, upper = lower.astype(F32), upper.astype(F32)
    hub_a = keep[:PADDED] + lower[:PADDED]
    own = keep[PADDED:FIRST] + lower[PADDED:] + upper[:PADDED]
    hub_b = keep[FIRST : 3 * PADDED] + upper[PADDED:]
    straight = ((z ^ (z >> 1)) & 1) == 0
    near, far = jnp.where(straight, hub_b, hub_a), jnp.where(straight, hub_a, hub_b)
    near, far = swap_z2(near.astype(BF), 0), swap_z2(far.astype(BF), 2)
    own = own + near.astype(F32) + far.astype(F32) + opposite.astype(F32)
    mine, other = own[:OWNED], own[OWNED:CHIP]
    came = swap_core(jnp.where(core == 0, other, mine))
    mine = jnp.where(core == 0, mine, other)
    grads = jnp.concatenate(
        [jnp.where(core == 0, mine, came), jnp.where(core == 0, came, mine)], axis=1
    )

    grads = (grads * scale)[None]
    new_first = 0.9 * first_moment + 0.1 * grads
    new_second = 0.999 * second_moment + 0.001 * grads * grads
    update = (
        new_first / (1.0 - 0.9**10) / (jnp.sqrt(new_second / (1.0 - 0.999**10)) + 1e-08)
    ).astype(BF)[0]

    around = [update]
    for m, more in ((1, 0), (2, 5), (3, 21)):
        around.append(swap_y(jnp.pad(update, ((0, more), (0, 0))), m)[:OWNED])
    ordered = jnp.stack([lax.select_n(y ^ a, *around) for a in range(NY)], axis=1)
    rows = lax.optimization_barrier(ordered.reshape(-1, ordered.shape[2]))
    change = dot(rows, basis[0].T).reshape(OWNED, NY, -1)
    return (new_first, new_second, change.astype(BF).transpose(2, 1, 0)[None])


def solution(mesh):
    return jax.shard_map(
        local,
        mesh=mesh,
        in_specs=(
            P(None, "dp", "tensor"),
            P(None, "dp", "tensor"),
            P(None, "tensor", None),
            P(None, ("tensor", "dp"), None),
            P(None, ("tensor", "dp"), None),
        ),
        out_specs=(
            P(None, ("tensor", "dp"), None),
            P(None, ("tensor", "dp"), None),
            P(None, "tensor", None, "dp"),
        ),
        check_vma=False,
    )
```

```python
import jax
import jax.numpy as jnp
from jax import lax
from jax.experimental import pallas as pl
from jax.experimental.layout import Layout, with_layout_constraint
from jax.experimental.pallas import tpu as pltpu
from jax.sharding import PartitionSpec as P

NX, NZ, NCORE, NY = 4, 8, 2, 4
OWNED = 43
CHIP, PADDED = NCORE * OWNED, 88
BF, F32 = jnp.bfloat16, jnp.float32

Z_ORDER = (3, 1, -1, -3, -2, 0, 2, 4)
FIRST, HALF = 2 * PADDED, 4 * PADDED
X_ORDER = ((2, 1, 3, 0), (2, 3, 1, 0))
PAIRS = ((1, 3), (3, 1))


def send(value, move):
    pairs = []
    for d in range(NX * NZ * NCORE * NY):
        x, z, c, y = d // (NZ * NCORE * NY), d // (NCORE * NY) % NZ, d // NY % NCORE, d % NY
        x, z, c, y = move(x, z, c, y)
        pairs.append((d, ((x * NZ + z) * NCORE + c) * NY + y))
    value = with_layout_constraint(value, Layout(major_to_minor=(0, 1)))
    return lax.ppermute(value, ("dp", "tensor"), pairs)


def swap_core(value):
    return send(value, lambda x, z, c, y: (x, z, 1 - c, y))


def swap_x(value, m):
    return send(value, lambda x, z, c, y: (x ^ m, z, c, y))


def swap_z(value, k):
    return send(value, lambda x, z, c, y: (x, (z + k * (1 - 2 * (z % 2))) % NZ, c, y))


def swap_z2(value, shift):
    return send(value, lambda x, z, c, y: (x, ((z + shift) % NZ ^ 2) - shift & (NZ - 1), c, y))


def swap_y(value, m):
    return send(value, lambda x, z, c, y: (x, z, c, y ^ m))


def arrange_kernel(order_ref, own, came, *refs):
    outs, blocks = refs[:-1], refs[-1]
    rows, tokens = own.shape
    for s, source in enumerate((own, came)):
        for n in range(NX * NZ):
            start = n * CHIP
            low = start // 16 * 16
            high = min(rows, -(-(start + PADDED) // 16) * 16)
            piece = source[low:high, :].astype(F32)
            piece = piece[start - low : min(start - low + PADDED, high - low), :]
            if piece.shape[0] < PADDED:
                fill = jnp.zeros((PADDED - piece.shape[0], tokens), F32)
                piece = jnp.concatenate([piece, fill], axis=0)
            blocks[n, :, s * tokens : (s + 1) * tokens] = piece
    k = 0
    for out in outs:
        for i in range(0, out.shape[0], 2 * PADDED):
            pair = [blocks[order_ref[k + j]] for j in range(2)]
            out[i : i + 2 * PADDED, :] = jnp.concatenate(pair, axis=0).astype(BF)
            k += 2


def arrange(order, own, came):
    tokens = own.shape[1]
    shape = jax.ShapeDtypeStruct((2 * HALF, NCORE * tokens), BF)
    vmem = pl.BlockSpec(memory_space=pltpu.VMEM)
    smem = pl.BlockSpec(memory_space=pltpu.SMEM)
    return pl.pallas_call(
        arrange_kernel,
        out_shape=[shape] * 4,
        in_specs=[smem, vmem, vmem],
        out_specs=[vmem] * 4,
        scratch_shapes=[pltpu.VMEM((NX * NZ, PADDED, NCORE * tokens), F32)],
        compiler_params=pltpu.CompilerParams(vmem_limit_bytes=20 * 1024 * 1024),
        cost_estimate=pl.CostEstimate(flops=0, bytes_accessed=8 * 1024 * 1024, transcendentals=0),
    )(order, own, came)


def project_kernel(core_ref, features, basis, own, theirs):
    lanes = own.shape[1]
    total = jnp.dot(features[...], basis[...], preferred_element_type=F32)
    halves = total[:, :lanes], total[:, lanes:]
    for core in range(NCORE):

        @pl.when(core_ref[0] == core)
        def _(core=core):
            own[...] = halves[core]
            theirs[...] = halves[1 - core].astype(BF)


def project(core, features, basis):
    shape = features.shape[0], basis.shape[1] // NCORE
    vmem = pl.BlockSpec(memory_space=pltpu.VMEM)
    return pl.pallas_call(
        project_kernel,
        out_shape=[jax.ShapeDtypeStruct(shape, dtype) for dtype in (F32, BF)],
        in_specs=[pl.BlockSpec(memory_space=pltpu.SMEM), vmem, vmem],
        out_specs=[vmem] * 2,
        compiler_params=pltpu.CompilerParams(vmem_limit_bytes=8 * 1024 * 1024),
        cost_estimate=pl.CostEstimate(
            flops=2 * features.size * basis.shape[1], bytes_accessed=2 * 1024 * 1024, transcendentals=0
        ),
    )(core, features, basis)


def dot(a, b):
    out = lax.dot_general(a, b, (((1,), (0,)), ((), ())), preferred_element_type=F32)
    return with_layout_constraint(out, Layout(major_to_minor=(0, 1)))


def local(features, cotangent, basis, first_moment, second_moment):
    scale = 1.0 / (features.shape[1] * lax.axis_size("dp"))
    dp = lax.axis_index("dp")
    core, z, x = dp & 1, (dp >> 1) & (NZ - 1), dp >> 4
    y = lax.axis_index("tensor")

    up = 1 - 2 * (z & 1)
    blocks_z = (z + up * jnp.array(Z_ORDER, jnp.int32)) & (NZ - 1)
    blocks_z = blocks_z.reshape(2, 1, NZ // 2)
    blocks_x = (x ^ jnp.array(X_ORDER, jnp.int32)) * NZ
    order = (blocks_x[:, :, None] + blocks_z).reshape(-1)

    mine, theirs = project(core.reshape(1), features[0], basis[0])
    columns = cotangent[0].T
    other_columns = swap_core(columns)
    theirs = swap_core(theirs)
    came = [swap_y(p, m[0]) for p, m in zip((mine.astype(BF), theirs), PAIRS)]
    chunks = [p.astype(F32) + c.astype(F32) for p, c in zip((mine, theirs), came)]
    came = [swap_y(p.astype(BF), m[1]) for p, m in zip(chunks, PAIRS)]
    parts = arrange(order, columns, other_columns)
    came[1], parts = lax.optimization_barrier((came[1], parts))
    chunks = [p + c.astype(F32) for p, c in zip(chunks, came)]
    projected = jnp.concatenate([p.astype(BF) for p in chunks], axis=0)

    sent = [dot(part, projected).astype(BF) for part in parts[::2]]
    came = [swap_x(value, m[0]) for value, m in zip(sent, PAIRS)]
    projected, sent[1] = lax.optimization_barrier((projected, sent[1]))
    kept = lax.optimization_barrier([dot(part, projected) for part in parts[1::2]])
    kept = [k + c.astype(F32) for k, c in zip(kept, came)]
    came = [swap_x(k[:HALF].astype(BF), m[1]) for k, m in zip(kept, PAIRS)]
    leave, keep = [k[HALF:] + c.astype(F32) for k, c in zip(kept, came)]
    lower, upper = swap_z(leave[:FIRST].astype(BF), 1), swap_z(leave[FIRST:].astype(BF), -1)
    opposite = swap_z(keep[3 * PADDED :].astype(BF), 4)
    lower, upper = lower.astype(F32), upper.astype(F32)
    hub_a = keep[:PADDED] + lower[:PADDED]
    own = keep[PADDED:FIRST] + lower[PADDED:] + upper[:PADDED]
    hub_b = keep[FIRST : 3 * PADDED] + upper[PADDED:]
    straight = ((z ^ (z >> 1)) & 1) == 0
    near, far = jnp.where(straight, hub_b, hub_a), jnp.where(straight, hub_a, hub_b)
    near, far = swap_z2(near.astype(BF), 0), swap_z2(far.astype(BF), 2)
    own = own + near.astype(F32) + far.astype(F32) + opposite.astype(F32)
    mine, other = own[:OWNED], own[OWNED:CHIP]
    came = swap_core(jnp.where(core == 0, other, mine))
    mine = jnp.where(core == 0, mine, other)
    grads = jnp.concatenate(
        [jnp.where(core == 0, mine, came), jnp.where(core == 0, came, mine)], axis=1
    )

    grads = (grads * scale)[None]
    new_first = 0.9 * first_moment + 0.1 * grads
    new_second = 0.999 * second_moment + 0.001 * grads * grads
    update = (
        new_first / (1.0 - 0.9**10) / (jnp.sqrt(new_second / (1.0 - 0.999**10)) + 1e-08)
    ).astype(BF)[0]

    around = [update]
    for m, more in ((1, 0), (2, 5), (3, 21)):
        around.append(swap_y(jnp.pad(update, ((0, more), (0, 0))), m)[:OWNED])
    ordered = jnp.stack([lax.select_n(y ^ a, *around) for a in range(NY)], axis=1)
    rows = lax.optimization_barrier(ordered.reshape(-1, ordered.shape[2]))
    change = dot(rows, basis[0].T).reshape(OWNED, NY, -1)
    return (new_first, new_second, change.astype(BF).transpose(2, 1, 0)[None])


def solution(mesh):
    return jax.shard_map(
        local,
        mesh=mesh,
        in_specs=(
            P(None, "dp", "tensor"),
            P(None, "dp", "tensor"),
            P(None, "tensor", None),
            P(None, ("tensor", "dp"), None),
            P(None, ("tensor", "dp"), None),
        ),
        out_specs=(
            P(None, ("tensor", "dp"), None),
            P(None, ("tensor", "dp"), None),
            P(None, "tensor", None, "dp"),
        ),
        check_vma=False,
    )
```

```python
import jax
import jax.numpy as jnp
from jax import lax
from jax.experimental import pallas as pl
from jax.experimental.layout import Layout, with_layout_constraint
from jax.experimental.pallas import tpu as pltpu
from jax.sharding import PartitionSpec as P

NX, NZ, NCORE, NY = 4, 8, 2, 4
OWNED = 43
PIECES = 4
CHIP, PADDED = NCORE * OWNED, 88
BF, F32 = jnp.bfloat16, jnp.float32

Z_ORDER = (3, 1, -1, -3, -2, 0, 2, 4)
FIRST, HALF = 2 * PADDED, 4 * PADDED
X_ORDER = ((2, 1, 3, 0), (2, 3, 1, 0))
PAIRS = ((1, 3), (3, 1))


def send(value, move):
    pairs = []
    for d in range(NX * NZ * NCORE * NY):
        x, z, c, y = d // (NZ * NCORE * NY), d // (NCORE * NY) % NZ, d // NY % NCORE, d % NY
        x, z, c, y = move(x, z, c, y)
        pairs.append((d, ((x * NZ + z) * NCORE + c) * NY + y))
    value = with_layout_constraint(value, Layout(major_to_minor=(0, 1)))
    return lax.ppermute(value, ("dp", "tensor"), pairs)


def swap_core(value):
    return send(value, lambda x, z, c, y: (x, z, 1 - c, y))


def swap_x(value, m):
    return send(value, lambda x, z, c, y: (x ^ m, z, c, y))


def swap_z(value, k):
    return send(value, lambda x, z, c, y: (x, (z + k * (1 - 2 * (z % 2))) % NZ, c, y))


def swap_z2(value, shift):
    return send(value, lambda x, z, c, y: (x, ((z + shift) % NZ ^ 2) - shift & (NZ - 1), c, y))


def swap_y(value, m):
    return send(value, lambda x, z, c, y: (x, z, c, y ^ m))


def arrange_kernel(order_ref, own, came, *refs):
    outs, blocks = refs[:-1], refs[-1]
    rows, tokens = own.shape
    for s, source in enumerate((own, came)):
        for n in range(NX * NZ):
            start = n * CHIP
            low = start // 16 * 16
            high = min(rows, -(-(start + PADDED) // 16) * 16)
            piece = source[low:high, :].astype(F32)
            piece = piece[start - low : min(start - low + PADDED, high - low), :]
            if piece.shape[0] < PADDED:
                fill = jnp.zeros((PADDED - piece.shape[0], tokens), F32)
                piece = jnp.concatenate([piece, fill], axis=0)
            blocks[n, :, s * tokens : (s + 1) * tokens] = piece
    k = 0
    for out in outs:
        for i in range(0, out.shape[0], 2 * PADDED):
            pair = [blocks[order_ref[k + j]] for j in range(2)]
            out[i : i + 2 * PADDED, :] = jnp.concatenate(pair, axis=0).astype(BF)
            k += 2


def arrange(order, own, came):
    tokens = own.shape[1]
    shape = jax.ShapeDtypeStruct((2 * HALF, NCORE * tokens), BF)
    vmem = pl.BlockSpec(memory_space=pltpu.VMEM)
    smem = pl.BlockSpec(memory_space=pltpu.SMEM)
    return pl.pallas_call(
        arrange_kernel,
        out_shape=[shape] * 4,
        in_specs=[smem, vmem, vmem],
        out_specs=[vmem] * 4,
        scratch_shapes=[pltpu.VMEM((NX * NZ, PADDED, NCORE * tokens), F32)],
        compiler_params=pltpu.CompilerParams(vmem_limit_bytes=20 * 1024 * 1024),
        cost_estimate=pl.CostEstimate(flops=0, bytes_accessed=8 * 1024 * 1024, transcendentals=0),
    )(order, own, came)


def project_kernel(core_ref, features, basis, own, theirs, f_buf, b_buf, total, sems):
    pieces, tokens, depth = f_buf.shape
    lanes = own.shape[1]
    copies = []
    for k in range(pieces):
        part = pl.ds(k * depth, depth)
        copies.append(pltpu.make_async_copy(features.at[:, part], f_buf.at[k], sems.at[0, k]))
        copies.append(pltpu.make_async_copy(basis.at[part, :], b_buf.at[k], sems.at[1, k]))
    for copy in copies:
        copy.start()
    for k in range(pieces):
        copies[2 * k].wait()
        copies[2 * k + 1].wait()
        term = jnp.dot(f_buf[k], b_buf[k], preferred_element_type=F32)
        total[...] = term if k == 0 else total[...] + term
    for core in range(NCORE):

        @pl.when(core_ref[0] == core)
        def _(core=core):
            own[...] = total[:, core * lanes : (core + 1) * lanes]
            theirs[...] = total[:, (1 - core) * lanes : (2 - core) * lanes].astype(BF)


def project(core, features, basis):
    tokens, depth = features.shape
    rank = basis.shape[1]
    step = depth // PIECES
    vmem = pl.BlockSpec(memory_space=pltpu.VMEM)
    hbm = pl.BlockSpec(memory_space=pltpu.HBM)
    return pl.pallas_call(
        project_kernel,
        out_shape=[
            jax.ShapeDtypeStruct((tokens, rank // NCORE), F32),
            jax.ShapeDtypeStruct((tokens, rank // NCORE), BF),
        ],
        in_specs=[pl.BlockSpec(memory_space=pltpu.SMEM), hbm, hbm],
        out_specs=[vmem] * 2,
        scratch_shapes=[
            pltpu.VMEM((PIECES, tokens, step), BF),
            pltpu.VMEM((PIECES, step, rank), BF),
            pltpu.VMEM((tokens, rank), F32),
            pltpu.SemaphoreType.DMA((2, PIECES)),
        ],
        compiler_params=pltpu.CompilerParams(vmem_limit_bytes=60 * 1024 * 1024),
        cost_estimate=pl.CostEstimate(
            flops=2 * tokens * depth * rank, bytes_accessed=3 * 1024 * 1024, transcendentals=0
        ),
    )(core, features, basis)


def dot(a, b):
    out = lax.dot_general(a, b, (((1,), (0,)), ((), ())), preferred_element_type=F32)
    return with_layout_constraint(out, Layout(major_to_minor=(0, 1)))


def local(features, cotangent, basis, first_moment, second_moment):
    scale = 1.0 / (features.shape[1] * lax.axis_size("dp"))
    dp = lax.axis_index("dp")
    core, z, x = dp & 1, (dp >> 1) & (NZ - 1), dp >> 4
    y = lax.axis_index("tensor")

    up = 1 - 2 * (z & 1)
    blocks_z = (z + up * jnp.array(Z_ORDER, jnp.int32)) & (NZ - 1)
    blocks_z = blocks_z.reshape(2, 1, NZ // 2)
    blocks_x = (x ^ jnp.array(X_ORDER, jnp.int32)) * NZ
    order = (blocks_x[:, :, None] + blocks_z).reshape(-1)

    mine, theirs = project(core.reshape(1), features[0], basis[0])
    columns = cotangent[0].T
    other_columns = swap_core(columns)
    theirs = swap_core(theirs)
    mine = lax.optimization_barrier(mine.astype(BF))
    came = [swap_y(p, m[0]) for p, m in zip((mine, theirs), PAIRS)]
    chunks = [p.astype(F32) + c.astype(F32) for p, c in zip((mine, theirs), came)]
    came = [swap_y(p.astype(BF), m[1]) for p, m in zip(chunks, PAIRS)]
    parts = arrange(order, columns, other_columns)
    came[1], parts = lax.optimization_barrier((came[1], parts))
    chunks = [p + c.astype(F32) for p, c in zip(chunks, came)]
    projected = jnp.concatenate([p.astype(BF) for p in chunks], axis=0)

    sent = [dot(part, projected).astype(BF) for part in parts[::2]]
    came = [swap_x(value, m[0]) for value, m in zip(sent, PAIRS)]
    projected, sent[1] = lax.optimization_barrier((projected, sent[1]))
    kept = lax.optimization_barrier([dot(part, projected) for part in parts[1::2]])
    kept = [k + c.astype(F32) for k, c in zip(kept, came)]
    came = [swap_x(k[:HALF].astype(BF), m[1]) for k, m in zip(kept, PAIRS)]
    leave, keep = [k[HALF:] + c.astype(F32) for k, c in zip(kept, came)]
    lower, upper = swap_z(leave[:FIRST].astype(BF), 1), swap_z(leave[FIRST:].astype(BF), -1)
    opposite = swap_z(keep[3 * PADDED :].astype(BF), 4)
    lower, upper = lower.astype(F32), upper.astype(F32)
    hub_a = keep[:PADDED] + lower[:PADDED]
    own = keep[PADDED:FIRST] + lower[PADDED:] + upper[:PADDED]
    hub_b = keep[FIRST : 3 * PADDED] + upper[PADDED:]
    straight = ((z ^ (z >> 1)) & 1) == 0
    near, far = jnp.where(straight, hub_b, hub_a), jnp.where(straight, hub_a, hub_b)
    near, far = swap_z2(near.astype(BF), 0), swap_z2(far.astype(BF), 2)
    own = own + near.astype(F32) + far.astype(F32) + opposite.astype(F32)
    mine, other = own[:OWNED], own[OWNED:CHIP]
    came = swap_core(jnp.where(core == 0, other, mine))
    mine = jnp.where(core == 0, mine, other)
    grads = jnp.concatenate(
        [jnp.where(core == 0, mine, came), jnp.where(core == 0, came, mine)], axis=1
    )

    grads = (grads * scale)[None]
    new_first = 0.9 * first_moment + 0.1 * grads
    new_second = 0.999 * second_moment + 0.001 * grads * grads
    update = (
        new_first / (1.0 - 0.9**10) / (jnp.sqrt(new_second / (1.0 - 0.999**10)) + 1e-08)
    ).astype(BF)[0]

    around = [update]
    for m, more in ((1, 0), (2, 5), (3, 21)):
        around.append(swap_y(jnp.pad(update, ((0, more), (0, 0))), m)[:OWNED])
    ordered = jnp.stack([lax.select_n(y ^ a, *around) for a in range(NY)], axis=1)
    rows = lax.optimization_barrier(ordered.reshape(-1, ordered.shape[2]))
    change = dot(rows, basis[0].T).reshape(OWNED, NY, -1)
    return (new_first, new_second, change.astype(BF).transpose(2, 1, 0)[None])


def solution(mesh):
    return jax.shard_map(
        local,
        mesh=mesh,
        in_specs=(
            P(None, "dp", "tensor"),
            P(None, "dp", "tensor"),
            P(None, "tensor", None),
            P(None, ("tensor", "dp"), None),
            P(None, ("tensor", "dp"), None),
        ),
        out_specs=(
            P(None, ("tensor", "dp"), None),
            P(None, ("tensor", "dp"), None),
            P(None, "tensor", None, "dp"),
        ),
        check_vma=False,
    )
```

```python
import jax
import jax.numpy as jnp
from jax import lax
from jax.experimental import pallas as pl
from jax.experimental.layout import Layout, with_layout_constraint
from jax.experimental.pallas import tpu as pltpu
from jax.sharding import PartitionSpec as P

NX, NZ, NCORE, NY = 4, 8, 2, 4
OWNED = 43
PIECES = 4
CHIP, PADDED = NCORE * OWNED, 88
BF, F32 = jnp.bfloat16, jnp.float32

Z_ORDER = (3, 1, -1, -3, -2, 0, 2, 4)
FIRST, HALF = 2 * PADDED, 4 * PADDED
X_ORDER = ((2, 1, 3, 0), (2, 3, 1, 0))
PAIRS = ((1, 3), (3, 1))


def send(value, move):
    pairs = []
    for d in range(NX * NZ * NCORE * NY):
        x, z, c, y = d // (NZ * NCORE * NY), d // (NCORE * NY) % NZ, d // NY % NCORE, d % NY
        x, z, c, y = move(x, z, c, y)
        pairs.append((d, ((x * NZ + z) * NCORE + c) * NY + y))
    value = with_layout_constraint(value, Layout(major_to_minor=(0, 1)))
    return lax.ppermute(value, ("dp", "tensor"), pairs)


def swap_core(value):
    return send(value, lambda x, z, c, y: (x, z, 1 - c, y))


def swap_x(value, m):
    return send(value, lambda x, z, c, y: (x ^ m, z, c, y))


def swap_z(value, k):
    return send(value, lambda x, z, c, y: (x, (z + k * (1 - 2 * (z % 2))) % NZ, c, y))


def swap_z2(value, shift):
    return send(value, lambda x, z, c, y: (x, ((z + shift) % NZ ^ 2) - shift & (NZ - 1), c, y))


def swap_y(value, m):
    return send(value, lambda x, z, c, y: (x, z, c, y ^ m))


def arrange_kernel(order_ref, own, came, *refs):
    outs, blocks = refs[:-1], refs[-1]
    rows, tokens = own.shape
    for s, source in enumerate((own, came)):
        for n in range(NX * NZ):
            start = n * CHIP
            low = start // 16 * 16
            high = min(rows, -(-(start + PADDED) // 16) * 16)
            piece = source[low:high, :].astype(F32)
            piece = piece[start - low : min(start - low + PADDED, high - low), :]
            if piece.shape[0] < PADDED:
                fill = jnp.zeros((PADDED - piece.shape[0], tokens), F32)
                piece = jnp.concatenate([piece, fill], axis=0)
            blocks[n, :, s * tokens : (s + 1) * tokens] = piece
    k = 0
    for out in outs:
        for i in range(0, out.shape[0], 2 * PADDED):
            pair = [blocks[order_ref[k + j]] for j in range(2)]
            out[i : i + 2 * PADDED, :] = jnp.concatenate(pair, axis=0).astype(BF)
            k += 2


def arrange(order, own, came):
    tokens = own.shape[1]
    shape = jax.ShapeDtypeStruct((2 * HALF, NCORE * tokens), BF)
    vmem = pl.BlockSpec(memory_space=pltpu.VMEM)
    smem = pl.BlockSpec(memory_space=pltpu.SMEM)
    return pl.pallas_call(
        arrange_kernel,
        out_shape=[shape] * 4,
        in_specs=[smem, vmem, vmem],
        out_specs=[vmem] * 4,
        scratch_shapes=[pltpu.VMEM((NX * NZ, PADDED, NCORE * tokens), F32)],
        compiler_params=pltpu.CompilerParams(vmem_limit_bytes=20 * 1024 * 1024),
        cost_estimate=pl.CostEstimate(flops=0, bytes_accessed=8 * 1024 * 1024, transcendentals=0),
    )(order, own, came)


def project_kernel(core_ref, features, basis, own, theirs, f_buf, b_buf, total, sems):
    pieces, tokens, depth = f_buf.shape
    lanes = own.shape[1]
    copies = []
    for k in range(pieces):
        part = pl.ds(k * depth, depth)
        copies.append(pltpu.make_async_copy(features.at[:, part], f_buf.at[k], sems.at[0, k]))
        copies.append(pltpu.make_async_copy(basis.at[part, :], b_buf.at[k], sems.at[1, k]))
    for copy in copies:
        copy.start()
    for k in range(pieces):
        copies[2 * k].wait()
        copies[2 * k + 1].wait()
        term = jnp.dot(f_buf[k], b_buf[k], preferred_element_type=F32)
        total[...] = term if k == 0 else total[...] + term
    for core in range(NCORE):

        @pl.when(core_ref[0] == core)
        def _(core=core):
            own[...] = total[:, core * lanes : (core + 1) * lanes].astype(BF)
            theirs[...] = total[:, (1 - core) * lanes : (2 - core) * lanes].astype(BF)


def project(core, features, basis):
    tokens, depth = features.shape
    rank = basis.shape[1]
    step = depth // PIECES
    vmem = pl.BlockSpec(memory_space=pltpu.VMEM)
    hbm = pl.BlockSpec(memory_space=pltpu.HBM)
    return pl.pallas_call(
        project_kernel,
        out_shape=[jax.ShapeDtypeStruct((tokens, rank // NCORE), BF)] * 2,
        in_specs=[pl.BlockSpec(memory_space=pltpu.SMEM), hbm, hbm],
        out_specs=[vmem] * 2,
        scratch_shapes=[
            pltpu.VMEM((PIECES, tokens, step), BF),
            pltpu.VMEM((PIECES, step, rank), BF),
            pltpu.VMEM((tokens, rank), F32),
            pltpu.SemaphoreType.DMA((2, PIECES)),
        ],
        compiler_params=pltpu.CompilerParams(vmem_limit_bytes=60 * 1024 * 1024),
        cost_estimate=pl.CostEstimate(
            flops=2 * tokens * depth * rank, bytes_accessed=3 * 1024 * 1024, transcendentals=0
        ),
    )(core, features, basis)


def dot(a, b):
    out = lax.dot_general(a, b, (((1,), (0,)), ((), ())), preferred_element_type=F32)
    return with_layout_constraint(out, Layout(major_to_minor=(0, 1)))


def local(features, cotangent, basis, first_moment, second_moment):
    scale = 1.0 / (features.shape[1] * lax.axis_size("dp"))
    dp = lax.axis_index("dp")
    core, z, x = dp & 1, (dp >> 1) & (NZ - 1), dp >> 4
    y = lax.axis_index("tensor")

    up = 1 - 2 * (z & 1)
    blocks_z = (z + up * jnp.array(Z_ORDER, jnp.int32)) & (NZ - 1)
    blocks_z = blocks_z.reshape(2, 1, NZ // 2)
    blocks_x = (x ^ jnp.array(X_ORDER, jnp.int32)) * NZ
    order = (blocks_x[:, :, None] + blocks_z).reshape(-1)

    mine, theirs = project(core.reshape(1), features[0], basis[0])
    columns = cotangent[0].T
    other_columns = swap_core(columns)
    theirs = swap_core(theirs)
    came = [swap_y(p, m[0]) for p, m in zip((mine, theirs), PAIRS)]
    chunks = [p.astype(F32) + c.astype(F32) for p, c in zip((mine, theirs), came)]
    chunks[0] = lax.optimization_barrier(chunks[0])
    came = [swap_y(p.astype(BF), m[1]) for p, m in zip(chunks, PAIRS)]
    parts = arrange(order, columns, other_columns)
    came[1], parts = lax.optimization_barrier((came[1], parts))
    chunks = [p + c.astype(F32) for p, c in zip(chunks, came)]
    projected = jnp.concatenate([p.astype(BF) for p in chunks], axis=0)

    sent = [dot(part, projected).astype(BF) for part in parts[::2]]
    came = [swap_x(value, m[0]) for value, m in zip(sent, PAIRS)]
    projected, sent[1] = lax.optimization_barrier((projected, sent[1]))
    kept = lax.optimization_barrier([dot(part, projected) for part in parts[1::2]])
    kept = [k + c.astype(F32) for k, c in zip(kept, came)]
    came = [swap_x(k[:HALF].astype(BF), m[1]) for k, m in zip(kept, PAIRS)]
    leave, keep = [k[HALF:] + c.astype(F32) for k, c in zip(kept, came)]
    lower, upper = swap_z(leave[:FIRST].astype(BF), 1), swap_z(leave[FIRST:].astype(BF), -1)
    opposite = swap_z(keep[3 * PADDED :].astype(BF), 4)
    lower, upper = lower.astype(F32), upper.astype(F32)
    hub_a = keep[:PADDED] + lower[:PADDED]
    own = keep[PADDED:FIRST] + lower[PADDED:] + upper[:PADDED]
    hub_b = keep[FIRST : 3 * PADDED] + upper[PADDED:]
    straight = ((z ^ (z >> 1)) & 1) == 0
    near, far = jnp.where(straight, hub_b, hub_a), jnp.where(straight, hub_a, hub_b)
    near, far = swap_z2(near.astype(BF), 0), swap_z2(far.astype(BF), 2)
    own = own + near.astype(F32) + far.astype(F32) + opposite.astype(F32)
    mine, other = own[:OWNED], own[OWNED:CHIP]
    came = swap_core(jnp.where(core == 0, other, mine))
    mine = jnp.where(core == 0, mine, other)
    grads = jnp.concatenate(
        [jnp.where(core == 0, mine, came), jnp.where(core == 0, came, mine)], axis=1
    )

    grads = (grads * scale)[None]
    new_first = 0.9 * first_moment + 0.1 * grads
    new_second = 0.999 * second_moment + 0.001 * grads * grads
    update = (
        new_first / (1.0 - 0.9**10) / (jnp.sqrt(new_second / (1.0 - 0.999**10)) + 1e-08)
    ).astype(BF)[0]

    around = [update]
    for m, more in ((1, 0), (2, 5), (3, 21)):
        around.append(swap_y(jnp.pad(update, ((0, more), (0, 0))), m)[:OWNED])
    ordered = jnp.stack([lax.select_n(y ^ a, *around) for a in range(NY)], axis=1)
    rows = lax.optimization_barrier(ordered.reshape(-1, ordered.shape[2]))
    change = dot(rows, basis[0].T).reshape(OWNED, NY, -1)
    return (new_first, new_second, change.astype(BF).transpose(2, 1, 0)[None])


def solution(mesh):
    return jax.shard_map(
        local,
        mesh=mesh,
        in_specs=(
            P(None, "dp", "tensor"),
            P(None, "dp", "tensor"),
            P(None, "tensor", None),
            P(None, ("tensor", "dp"), None),
            P(None, ("tensor", "dp"), None),
        ),
        out_specs=(
            P(None, ("tensor", "dp"), None),
            P(None, ("tensor", "dp"), None),
            P(None, "tensor", None, "dp"),
        ),
        check_vma=False,
    )
```

```python
import jax
import jax.numpy as jnp
from jax import lax
from jax.experimental import pallas as pl
from jax.experimental.layout import Layout, with_layout_constraint
from jax.experimental.pallas import tpu as pltpu
from jax.sharding import PartitionSpec as P

NX, NZ, NCORE, NY = 4, 8, 2, 4
OWNED = 43
CHIP, PADDED = NCORE * OWNED, 88
BF, F32 = jnp.bfloat16, jnp.float32

Z_ORDER = (3, 1, -1, -3, -2, 0, 2, 4)
FIRST, HALF = 2 * PADDED, 4 * PADDED
X_ORDER = ((2, 1, 3, 0), (2, 3, 1, 0))
PAIRS = ((1, 3), (3, 1))


def send(value, move):
    pairs = []
    for d in range(NX * NZ * NCORE * NY):
        x, z, c, y = d // (NZ * NCORE * NY), d // (NCORE * NY) % NZ, d // NY % NCORE, d % NY
        x, z, c, y = move(x, z, c, y)
        pairs.append((d, ((x * NZ + z) * NCORE + c) * NY + y))
    value = with_layout_constraint(value, Layout(major_to_minor=(0, 1)))
    return lax.ppermute(value, ("dp", "tensor"), pairs)


def swap_core(value):
    return send(value, lambda x, z, c, y: (x, z, 1 - c, y))


def swap_x(value, m):
    return send(value, lambda x, z, c, y: (x ^ m, z, c, y))


def swap_z(value, k):
    return send(value, lambda x, z, c, y: (x, (z + k * (1 - 2 * (z % 2))) % NZ, c, y))


def swap_z2(value, shift):
    return send(value, lambda x, z, c, y: (x, ((z + shift) % NZ ^ 2) - shift & (NZ - 1), c, y))


def swap_y(value, m):
    return send(value, lambda x, z, c, y: (x, z, c, y ^ m))


def arrange_kernel(order_ref, own, came, *refs):
    outs, blocks = refs[:-1], refs[-1]
    rows, tokens = own.shape
    for s, source in enumerate((own, came)):
        for n in range(NX * NZ):
            start = n * CHIP
            low = start // 16 * 16
            high = min(rows, -(-(start + PADDED) // 16) * 16)
            piece = source[low:high, :].astype(F32)
            piece = piece[start - low : min(start - low + PADDED, high - low), :]
            if piece.shape[0] < PADDED:
                fill = jnp.zeros((PADDED - piece.shape[0], tokens), F32)
                piece = jnp.concatenate([piece, fill], axis=0)
            blocks[n, :, s * tokens : (s + 1) * tokens] = piece
    k = 0
    for out in outs:
        for i in range(0, out.shape[0], 2 * PADDED):
            pair = [blocks[order_ref[k + j]] for j in range(2)]
            out[i : i + 2 * PADDED, :] = jnp.concatenate(pair, axis=0).astype(BF)
            k += 2


def arrange(order, own, came):
    tokens = own.shape[1]
    shape = jax.ShapeDtypeStruct((2 * HALF, NCORE * tokens), BF)
    vmem = pl.BlockSpec(memory_space=pltpu.VMEM)
    smem = pl.BlockSpec(memory_space=pltpu.SMEM)
    return pl.pallas_call(
        arrange_kernel,
        out_shape=[shape] * 4,
        in_specs=[smem, vmem, vmem],
        out_specs=[vmem] * 4,
        scratch_shapes=[pltpu.VMEM((NX * NZ, PADDED, NCORE * tokens), F32)],
        compiler_params=pltpu.CompilerParams(vmem_limit_bytes=20 * 1024 * 1024),
        cost_estimate=pl.CostEstimate(flops=0, bytes_accessed=8 * 1024 * 1024, transcendentals=0),
    )(order, own, came)


def project_kernel(core_ref, features, basis, own, theirs):
    lanes = own.shape[1]
    total = jnp.dot(features[...], basis[...], preferred_element_type=F32)
    halves = total[:, :lanes], total[:, lanes:]
    for core in range(NCORE):

        @pl.when(core_ref[0] == core)
        def _(core=core):
            own[...] = halves[core]
            theirs[...] = halves[1 - core].astype(BF)


def project(core, features, basis):
    shape = features.shape[0], basis.shape[1] // NCORE
    vmem = pl.BlockSpec(memory_space=pltpu.VMEM)
    return pl.pallas_call(
        project_kernel,
        out_shape=[jax.ShapeDtypeStruct(shape, dtype) for dtype in (F32, BF)],
        in_specs=[pl.BlockSpec(memory_space=pltpu.SMEM), vmem, vmem],
        out_specs=[vmem] * 2,
        compiler_params=pltpu.CompilerParams(vmem_limit_bytes=8 * 1024 * 1024),
        cost_estimate=pl.CostEstimate(
            flops=2 * features.size * basis.shape[1], bytes_accessed=2 * 1024 * 1024, transcendentals=0
        ),
    )(core, features, basis)


def dot(a, b):
    out = lax.dot_general(a, b, (((1,), (0,)), ((), ())), preferred_element_type=F32)
    return with_layout_constraint(out, Layout(major_to_minor=(0, 1)))


def local(features, cotangent, basis, first_moment, second_moment):
    scale = 1.0 / (features.shape[1] * lax.axis_size("dp"))
    dp = lax.axis_index("dp")
    core, z, x = dp & 1, (dp >> 1) & (NZ - 1), dp >> 4
    y = lax.axis_index("tensor")

    up = 1 - 2 * (z & 1)
    blocks_z = (z + up * jnp.array(Z_ORDER, jnp.int32)) & (NZ - 1)
    blocks_z = blocks_z.reshape(2, 1, NZ // 2)
    blocks_x = (x ^ jnp.array(X_ORDER, jnp.int32)) * NZ
    order = (blocks_x[:, :, None] + blocks_z).reshape(-1)

    mine, theirs = project(core.reshape(1), features[0], basis[0])
    columns = cotangent[0].T
    other_columns = swap_core(columns)
    theirs = swap_core(theirs)
    came = [swap_y(p, m[0]) for p, m in zip((mine.astype(BF), theirs), PAIRS)]
    chunks = [p.astype(F32) + c.astype(F32) for p, c in zip((mine, theirs), came)]
    came = [swap_y(p.astype(BF), m[1]) for p, m in zip(chunks, PAIRS)]
    parts = arrange(order, columns, other_columns)
    came[1], parts = lax.optimization_barrier((came[1], parts))
    chunks = [p + c.astype(F32) for p, c in zip(chunks, came)]
    projected = jnp.concatenate([p.astype(BF) for p in chunks], axis=0)

    sent = [dot(parts[0], projected).astype(BF)]
    after, sent[0] = lax.optimization_barrier((projected, sent[0]))
    kept = [dot(parts[1], after)]
    after, kept[0] = lax.optimization_barrier((after, kept[0]))
    sent.append(dot(parts[2], after).astype(BF))
    came = [swap_x(value, m[0]) for value, m in zip(sent, PAIRS)]
    after, sent[1] = lax.optimization_barrier((after, sent[1]))
    kept.append(lax.optimization_barrier(dot(parts[3], after)))
    kept = [k + c.astype(F32) for k, c in zip(kept, came)]
    came = [swap_x(k[:HALF].astype(BF), m[1]) for k, m in zip(kept, PAIRS)]
    leave, keep = [k[HALF:] + c.astype(F32) for k, c in zip(kept, came)]
    lower, upper = swap_z(leave[:FIRST].astype(BF), 1), swap_z(leave[FIRST:].astype(BF), -1)
    opposite = swap_z(keep[3 * PADDED :].astype(BF), 4)
    lower, upper = lower.astype(F32), upper.astype(F32)
    hub_a = keep[:PADDED] + lower[:PADDED]
    own = keep[PADDED:FIRST] + lower[PADDED:] + upper[:PADDED]
    hub_b = keep[FIRST : 3 * PADDED] + upper[PADDED:]
    straight = ((z ^ (z >> 1)) & 1) == 0
    near, far = jnp.where(straight, hub_b, hub_a), jnp.where(straight, hub_a, hub_b)
    near, far = swap_z2(near.astype(BF), 0), swap_z2(far.astype(BF), 2)
    own = own + near.astype(F32) + far.astype(F32) + opposite.astype(F32)
    mine, other = own[:OWNED], own[OWNED:CHIP]
    came = swap_core(jnp.where(core == 0, other, mine))
    mine = jnp.where(core == 0, mine, other)
    grads = jnp.concatenate(
        [jnp.where(core == 0, mine, came), jnp.where(core == 0, came, mine)], axis=1
    )

    grads = (grads * scale)[None]
    new_first = 0.9 * first_moment + 0.1 * grads
    new_second = 0.999 * second_moment + 0.001 * grads * grads
    update = (
        new_first / (1.0 - 0.9**10) / (jnp.sqrt(new_second / (1.0 - 0.999**10)) + 1e-08)
    ).astype(BF)[0]

    around = [update]
    for m, more in ((1, 0), (2, 5), (3, 21)):
        around.append(swap_y(jnp.pad(update, ((0, more), (0, 0))), m)[:OWNED])
    ordered = jnp.stack([lax.select_n(y ^ a, *around) for a in range(NY)], axis=1)
    rows = lax.optimization_barrier(ordered.reshape(-1, ordered.shape[2]))
    change = dot(rows, basis[0].T).reshape(OWNED, NY, -1)
    return (new_first, new_second, change.astype(BF).transpose(2, 1, 0)[None])


def solution(mesh):
    return jax.shard_map(
        local,
        mesh=mesh,
        in_specs=(
            P(None, "dp", "tensor"),
            P(None, "dp", "tensor"),
            P(None, "tensor", None),
            P(None, ("tensor", "dp"), None),
            P(None, ("tensor", "dp"), None),
        ),
        out_specs=(
            P(None, ("tensor", "dp"), None),
            P(None, ("tensor", "dp"), None),
            P(None, "tensor", None, "dp"),
        ),
        check_vma=False,
    )
```

```python
import jax
import jax.numpy as jnp
from jax import lax
from jax.experimental import pallas as pl
from jax.experimental.layout import Layout, with_layout_constraint
from jax.experimental.pallas import tpu as pltpu
from jax.sharding import PartitionSpec as P

NX, NZ, NCORE, NY = 4, 8, 2, 4
OWNED = 43
CHIP, PADDED = NCORE * OWNED, 88
BF, F32 = jnp.bfloat16, jnp.float32

Z_ORDER = (3, 1, -1, -3, -2, 0, 2, 4)
FIRST, HALF = 2 * PADDED, 4 * PADDED
X_ORDER = ((2, 1, 3, 0), (2, 3, 1, 0))
PAIRS = ((1, 3), (3, 1))


def send(value, move):
    pairs = []
    for d in range(NX * NZ * NCORE * NY):
        x, z, c, y = d // (NZ * NCORE * NY), d // (NCORE * NY) % NZ, d // NY % NCORE, d % NY
        x, z, c, y = move(x, z, c, y)
        pairs.append((d, ((x * NZ + z) * NCORE + c) * NY + y))
    value = with_layout_constraint(value, Layout(major_to_minor=(0, 1)))
    return lax.ppermute(value, ("dp", "tensor"), pairs)


def swap_core(value):
    return send(value, lambda x, z, c, y: (x, z, 1 - c, y))


def swap_x(value, m):
    return send(value, lambda x, z, c, y: (x ^ m, z, c, y))


def swap_z(value, k):
    return send(value, lambda x, z, c, y: (x, (z + k * (1 - 2 * (z % 2))) % NZ, c, y))


def swap_z2(value, shift):
    return send(value, lambda x, z, c, y: (x, ((z + shift) % NZ ^ 2) - shift & (NZ - 1), c, y))


def swap_y(value, m):
    return send(value, lambda x, z, c, y: (x, z, c, y ^ m))


def arrange_kernel(order_ref, own, came, *refs):
    outs, blocks = refs[:-1], refs[-1]
    rows, tokens = own.shape
    for s, source in enumerate((own, came)):
        for n in range(NX * NZ):
            start = n * CHIP
            low = start // 16 * 16
            high = min(rows, -(-(start + PADDED) // 16) * 16)
            piece = source[low:high, :].astype(F32)
            piece = piece[start - low : min(start - low + PADDED, high - low), :]
            if piece.shape[0] < PADDED:
                fill = jnp.zeros((PADDED - piece.shape[0], tokens), F32)
                piece = jnp.concatenate([piece, fill], axis=0)
            blocks[n, :, s * tokens : (s + 1) * tokens] = piece
    k = 0
    for out in outs:
        for i in range(0, out.shape[0], 2 * PADDED):
            pair = [blocks[order_ref[k + j]] for j in range(2)]
            out[i : i + 2 * PADDED, :] = jnp.concatenate(pair, axis=0).astype(BF)
            k += 2


def arrange(order, own, came):
    tokens = own.shape[1]
    shape = jax.ShapeDtypeStruct((2 * HALF, NCORE * tokens), BF)
    vmem = pl.BlockSpec(memory_space=pltpu.VMEM)
    smem = pl.BlockSpec(memory_space=pltpu.SMEM)
    return pl.pallas_call(
        arrange_kernel,
        out_shape=[shape] * 4,
        in_specs=[smem, vmem, vmem],
        out_specs=[vmem] * 4,
        scratch_shapes=[pltpu.VMEM((NX * NZ, PADDED, NCORE * tokens), F32)],
        compiler_params=pltpu.CompilerParams(vmem_limit_bytes=20 * 1024 * 1024),
        cost_estimate=pl.CostEstimate(flops=0, bytes_accessed=8 * 1024 * 1024, transcendentals=0),
    )(order, own, came)


def project_kernel(core_ref, features, basis, own, theirs):
    lanes = own.shape[1]
    total = jnp.dot(features[...], basis[...], preferred_element_type=F32)
    halves = total[:, :lanes], total[:, lanes:]
    for core in range(NCORE):

        @pl.when(core_ref[0] == core)
        def _(core=core):
            own[...] = halves[core]
            theirs[...] = halves[1 - core].astype(BF)


def project(core, features, basis):
    shape = features.shape[0], basis.shape[1] // NCORE
    vmem = pl.BlockSpec(memory_space=pltpu.VMEM)
    return pl.pallas_call(
        project_kernel,
        out_shape=[jax.ShapeDtypeStruct(shape, dtype) for dtype in (F32, BF)],
        in_specs=[pl.BlockSpec(memory_space=pltpu.SMEM), vmem, vmem],
        out_specs=[vmem] * 2,
        compiler_params=pltpu.CompilerParams(vmem_limit_bytes=8 * 1024 * 1024),
        cost_estimate=pl.CostEstimate(
            flops=2 * features.size * basis.shape[1], bytes_accessed=2 * 1024 * 1024, transcendentals=0
        ),
    )(core, features, basis)


def back_project_kernel(rows, basis, out):
    wide = lax.dot_general(
        rows[...], basis[...], (((1,), (1,)), ((), ())), preferred_element_type=F32
    )
    for b in range(OWNED):
        out[b] = wide[b * NY : (b + 1) * NY].astype(BF)


def back_project(rows, basis):
    vmem = pl.BlockSpec(memory_space=pltpu.VMEM)
    return pl.pallas_call(
        back_project_kernel,
        out_shape=jax.ShapeDtypeStruct((OWNED, NY, basis.shape[0]), BF),
        in_specs=[vmem] * 2,
        out_specs=vmem,
        compiler_params=pltpu.CompilerParams(vmem_limit_bytes=8 * 1024 * 1024),
        cost_estimate=pl.CostEstimate(
            flops=2 * rows.size * basis.shape[0], bytes_accessed=2 * 1024 * 1024, transcendentals=0
        ),
    )(rows, basis)


def dot(a, b):
    out = lax.dot_general(a, b, (((1,), (0,)), ((), ())), preferred_element_type=F32)
    return with_layout_constraint(out, Layout(major_to_minor=(0, 1)))


def local(features, cotangent, basis, first_moment, second_moment):
    scale = 1.0 / (features.shape[1] * lax.axis_size("dp"))
    dp = lax.axis_index("dp")
    core, z, x = dp & 1, (dp >> 1) & (NZ - 1), dp >> 4
    y = lax.axis_index("tensor")

    up = 1 - 2 * (z & 1)
    blocks_z = (z + up * jnp.array(Z_ORDER, jnp.int32)) & (NZ - 1)
    blocks_z = blocks_z.reshape(2, 1, NZ // 2)
    blocks_x = (x ^ jnp.array(X_ORDER, jnp.int32)) * NZ
    order = (blocks_x[:, :, None] + blocks_z).reshape(-1)

    mine, theirs = project(core.reshape(1), features[0], basis[0])
    columns = cotangent[0].T
    other_columns = swap_core(columns)
    theirs = swap_core(theirs)
    came = [swap_y(p, m[0]) for p, m in zip((mine.astype(BF), theirs), PAIRS)]
    chunks = [p.astype(F32) + c.astype(F32) for p, c in zip((mine, theirs), came)]
    came = [swap_y(p.astype(BF), m[1]) for p, m in zip(chunks, PAIRS)]
    parts = arrange(order, columns, other_columns)
    came[1], parts = lax.optimization_barrier((came[1], parts))
    chunks = [p + c.astype(F32) for p, c in zip(chunks, came)]
    projected = jnp.concatenate([p.astype(BF) for p in chunks], axis=0)

    sent = [dot(parts[0], projected).astype(BF)]
    after, sent[0] = lax.optimization_barrier((projected, sent[0]))
    kept = [dot(parts[1], after)]
    after, kept[0] = lax.optimization_barrier((after, kept[0]))
    sent.append(dot(parts[2], after).astype(BF))
    came = [swap_x(value, m[0]) for value, m in zip(sent, PAIRS)]
    after, sent[1] = lax.optimization_barrier((after, sent[1]))
    kept.append(lax.optimization_barrier(dot(parts[3], after)))
    kept = [k + c.astype(F32) for k, c in zip(kept, came)]
    came = [swap_x(k[:HALF].astype(BF), m[1]) for k, m in zip(kept, PAIRS)]
    leave, keep = [k[HALF:] + c.astype(F32) for k, c in zip(kept, came)]
    lower, upper = swap_z(leave[:FIRST].astype(BF), 1), swap_z(leave[FIRST:].astype(BF), -1)
    opposite = swap_z(keep[3 * PADDED :].astype(BF), 4)
    lower, upper = lower.astype(F32), upper.astype(F32)
    hub_a = keep[:PADDED] + lower[:PADDED]
    own = keep[PADDED:FIRST] + lower[PADDED:] + upper[:PADDED]
    hub_b = keep[FIRST : 3 * PADDED] + upper[PADDED:]
    straight = ((z ^ (z >> 1)) & 1) == 0
    near, far = jnp.where(straight, hub_b, hub_a), jnp.where(straight, hub_a, hub_b)
    near, far = swap_z2(near.astype(BF), 0), swap_z2(far.astype(BF), 2)
    own = own + near.astype(F32) + far.astype(F32) + opposite.astype(F32)
    mine, other = own[:OWNED], own[OWNED:CHIP]
    came = swap_core(jnp.where(core == 0, other, mine))
    mine = jnp.where(core == 0, mine, other)
    grads = jnp.concatenate(
        [jnp.where(core == 0, mine, came), jnp.where(core == 0, came, mine)], axis=1
    )

    grads = (grads * scale)[None]
    new_first = 0.9 * first_moment + 0.1 * grads
    new_second = 0.999 * second_moment + 0.001 * grads * grads
    update = (
        new_first / (1.0 - 0.9**10) / (jnp.sqrt(new_second / (1.0 - 0.999**10)) + 1e-08)
    ).astype(BF)[0]

    around = [update]
    for m, more in ((1, 0), (2, 5), (3, 21)):
        around.append(swap_y(jnp.pad(update, ((0, more), (0, 0))), m)[:OWNED])
    ordered = jnp.stack([lax.select_n(y ^ a, *around) for a in range(NY)], axis=1)
    rows = lax.optimization_barrier(ordered.reshape(-1, ordered.shape[2]))
    change = back_project(rows, basis[0])
    return (new_first, new_second, change.transpose(2, 1, 0)[None])


def solution(mesh):
    return jax.shard_map(
        local,
        mesh=mesh,
        in_specs=(
            P(None, "dp", "tensor"),
            P(None, "dp", "tensor"),
            P(None, "tensor", None),
            P(None, ("tensor", "dp"), None),
            P(None, ("tensor", "dp"), None),
        ),
        out_specs=(
            P(None, ("tensor", "dp"), None),
            P(None, ("tensor", "dp"), None),
            P(None, "tensor", None, "dp"),
        ),
        check_vma=False,
    )
```
